256 devices in a mesh: ingest: 64 (over y, z, core), span: 4 (over x).
Axes of the slice: x: 4, y: 4, z: 8, core: 2. Of those that a mesh axis runs over, the one named last changes fastest.
Arguments:
- embeddings: bfloat16 [131072, 1024], P(('ingest', 'span')), may hold values from -6 to 6
- owner: int32 [131072, 1], P(('ingest', 'span')), may hold values from 0 to 63; in each aligned block of 512 rows (0 to 511, 512 to 1023, ...) at most 16 rows name the same one
- cluster: int32 [131072], P(('ingest', 'span')), may hold values from 0 to 63
Outputs:
- max_similarity: float32 [131072], P(('ingest', 'span'))
The draws below stay inside these ranges and needn't reach their ends.
Inputs may be any that keep to these rules, and one draw needn't show every extreme that they name: Among the rows of one device, at most 16 name the same owner group, and some device has exactly 16 for some group.
All inputs are finite; a program needn't handle non-finite values.
Results may differ from the reference program's by a relative error of at most 0.0013.
Values may be sent and summed in bfloat16 or wider, within the bound.
No kernel may reach another device: no remote copies, remote signals or barrier semaphores. Data moves between devices by JAX's collectives and lax.ppermute only.
A program may use at most 64 MiB of HBM per device.

```python
import math
import jax
import jax.numpy as jnp
import numpy as np
from jax import lax

D = 1024
R_DEV = 512
CL_DEV = 64
CAP = 16
BLOCK = 1024
ROWS = 131072
N_INGEST = 64
N_SPAN = 4


def draw_cluster(key, part):
    key = jax.random.fold_in(key, 7)
    common_key, rare_key = jax.random.split(key)
    half_ids = CL_DEV // 2
    common = jax.random.randint(common_key, (ROWS,), 0, half_ids, dtype=jnp.int32)
    ticket = jax.random.randint(rare_key, (ROWS,), 0, R_DEV * N_SPAN, dtype=jnp.int32)
    return jnp.where(ticket < CL_DEV - half_ids, half_ids + ticket, common).astype(jnp.int32)


def block_scale(own_key, extent, cuts, smallest, high):
    def one(dim, blocks):
        heights = jax.random.uniform(jax.random.fold_in(jax.random.fold_in(own_key, 6), dim), (blocks,), jnp.float32, smallest / len(cuts), high / len(cuts))
        return jnp.repeat(jnp.exp(heights), extent[dim] // blocks).reshape((-1,) + (1,) * (len(extent) - dim - 1))

    gain = one(*cuts[0])
    for cut in cuts[1:]:
        gain = gain * one(*cut)
    return gain


def routed_block(rng, own, number, rows, number_of, top, limit, skew):
    sequence = jax.random.permutation(rng, number_of)
    crowded, ordinary = portions_of(number_of, rows * top, limit, skew, True), portions_of(number_of, rows * top, limit, skew, False)
    places = jnp.arange(number_of)

    def named(sizes, offset_by):
        used = int((sizes > 0).sum())
        fixed = max(1, used // 4)
        moved = fixed + (places - fixed + offset_by * (used - fixed)) % max(1, number_of - fixed)
        return jnp.zeros((number_of,), jnp.int32).at[sequence[jnp.where(places < fixed, places, moved)]].set(jnp.asarray(sizes, jnp.int32))

    sizes = jnp.where(number % 4 == 0, named(crowded, number // 4), named(ordinary, number - number // 4 - 1))
    mixed = jax.random.permutation(jax.random.fold_in(own, 3), number_of)
    source_of, sink = mixed[0:number_of // 2 * 2:2], mixed[1:number_of // 2 * 2:2]
    room = jnp.minimum(sizes[source_of] - 1, limit - sizes[sink]) // 2
    room = jnp.where((source_of == sequence[0]) | (sink == sequence[0]) | (sizes[sink] == 0), 0, jnp.maximum(room, 0))
    moved = jax.random.randint(jax.random.fold_in(own, 4), (number_of // 2,), 0, 1 << 20) % (room + 1)
    sizes = sizes.at[source_of].add(-moved).at[sink].add(moved)
    items = jnp.searchsorted(jnp.cumsum(sizes), jnp.arange(rows * top), side="right").astype(jnp.int32)
    listing = items.reshape(top, rows).T
    listing = listing[jax.random.permutation(jax.random.fold_in(own, 1), rows)]
    offset_by = jax.random.randint(jax.random.fold_in(own, 2), (rows, 1), 0, top)
    return jnp.take_along_axis(listing, (jnp.arange(top)[None, :] + offset_by) % top, axis=1)


def portions_of(amount, total, reach, lean, full):
    weights = [(1 << 20) // math.isqrt(grade ** lean) + 1 for grade in range(1, amount + 1)]
    largest = reach if full else min(reach, max(-(-total // amount), total * weights[0] // sum(weights)))
    least = 1 if total - largest >= amount - 1 else 0
    counts, spare = [largest] + [least] * (amount - 1), total - largest - least * (amount - 1)
    while spare > 0:
        candidates = [i for i in range(1, amount) if counts[i] < largest] or [i for i in range(1, amount) if counts[i] < reach]
        pool, budget = sum([weights[i] for i in candidates]), spare
        for i in candidates:
            more = min(reach - counts[i], max(1, budget * weights[i] // pool), spare)
            counts[i] = counts[i] + more
            spare = spare - more
    return np.array(counts)


def gaussian(own_key, extent, scale, limit, shards=(), kind=jnp.bfloat16):
    drawn = jax.random.normal(own_key, extent, jnp.float32) * scale
    if len(shards) > 0:
        drawn = block_scale(own_key, extent, shards, -0.22, 0.18) * drawn
    return jnp.clip(drawn, min=-limit, max=limit).astype(kind)


def setup_inputs(seed: int = 0) -> dict:
    arg_keys = jax.random.split(jax.random.key(seed), 4)
    embeddings = gaussian(arg_keys[0], (ROWS, D), 1.0, 6.0, ((0, 256),))
    owner_keys = jax.random.split(jax.random.fold_in(arg_keys[1], 1), ROWS // R_DEV)
    owner_turns = jax.random.permutation(jax.random.fold_in(arg_keys[1], 3), ROWS // R_DEV)
    owner = jax.vmap(lambda own, number: routed_block(jax.random.fold_in(arg_keys[1], 2), own, number, R_DEV, N_INGEST, 1, CAP, 2))(owner_keys, owner_turns).reshape((ROWS, 1))
    cluster = draw_cluster(jax.random.fold_in(arg_keys[3], 71), 0)
    return dict(embeddings=embeddings, owner=owner, cluster=cluster)


epsilon = 1e-06

def place_rows(target, groups, capacity):
    onehot = (target[:, None] == jnp.arange(groups, dtype=jnp.int32)[None, :]).astype(jnp.int32)
    within = lax.optimization_barrier(jnp.sum((jnp.cumsum(onehot, axis=0) - onehot) * onehot, axis=1))
    return (target * capacity + within).astype(jnp.int32)

def reference(embeddings, owner, cluster):
    groups = N_INGEST
    spans = N_SPAN
    capacity = CAP
    slots_dev = BLOCK
    values = embeddings.astype(jnp.float32)
    squared = lax.optimization_barrier(jnp.sum(values * values, axis=1, keepdims=True))
    unit = (values * lax.rsqrt(squared + epsilon)).astype(jnp.bfloat16)
    unit = unit.reshape(groups * spans, R_DEV, D)
    target = owner[:, 0].reshape(groups * spans, R_DEV)
    labels = cluster.reshape(groups * spans, R_DEV)
    slot_index = jax.vmap(lambda t: place_rows(t, groups, capacity))(target)

    def fill_buffers(rows, slots, ids):
        row_buffer = jnp.zeros((slots_dev, D), jnp.bfloat16).at[slots].set(rows)
        id_buffer = jnp.full((slots_dev,), -1, jnp.int32).at[slots].set(ids)
        return (row_buffer, id_buffer)
    row_buffer, id_buffer = jax.vmap(fill_buffers)(unit, slot_index, labels)
    row_buffer = row_buffer.reshape(groups, spans, groups, capacity, D).transpose(2, 1, 0, 3, 4)
    row_buffer = row_buffer.reshape(groups, spans * slots_dev, D)
    id_buffer = id_buffer.reshape(groups, spans, groups, capacity).transpose(2, 1, 0, 3)
    id_buffer = id_buffer.reshape(groups, spans * slots_dev)

    def group_max(inputs):
        rows, ids = inputs
        rows_wide = rows.astype(jnp.float32)
        scores = jnp.dot(rows_wide, rows_wide.T, precision=lax.Precision.HIGHEST, preferred_element_type=jnp.float32)
        position = jnp.arange(ids.shape[0], dtype=jnp.int32)
        same_cluster = (ids[:, None] == ids[None, :]) & (ids[:, None] >= 0) & (position[:, None] != position[None, :])
        return lax.optimization_barrier(jnp.max(jnp.where(same_cluster, scores, jnp.float32(-1.0)), axis=1))
    highest = lax.map(group_max, (row_buffer, id_buffer))
    highest = highest.reshape(groups, spans, groups, capacity).transpose(2, 1, 0, 3)
    highest = highest.reshape(groups * spans, slots_dev)
    result = jnp.take_along_axis(highest, slot_index, axis=1)
    return result.reshape(-1)
```

```python
import functools

import jax
import jax.numpy as jnp
from jax import lax
from jax.experimental import pallas as pl
from jax.experimental.pallas import tpu as pltpu
from jax.sharding import PartitionSpec as P

epsilon = 1e-06
capacity = 16
lanes = 128
cuts = (640, 384)
contract_last = (((1,), (1,)), ((), ()))
contract_first = (((1,), (0,)), ((), ()))


def params():
    return pltpu.CompilerParams(vmem_limit_bytes=40 * 1024 * 1024)


def rank_rows(owner, groups):
    rows = owner.shape[1]
    belongs = lax.broadcasted_iota(jnp.int32, (groups, rows), 0) == owner
    onehot = belongs.astype(jnp.bfloat16)
    earlier = lax.broadcasted_iota(jnp.int32, (rows, rows), 0) < lax.broadcasted_iota(
        jnp.int32, (rows, rows), 1
    )
    before = lax.dot_general(
        onehot, earlier.astype(jnp.bfloat16), contract_first, preferred_element_type=jnp.float32
    )
    within = jnp.sum(jnp.where(belongs, before, 0.0), axis=0, keepdims=True)
    return onehot, within


def place_kernel(groups, emb_ref, owner_ref, cluster_ref, *out_refs):
    *send_refs, ids_ref = out_refs
    owner = owner_ref[...]
    rows = owner.shape[1]
    onehot, within = rank_rows(owner, groups)
    values = emb_ref[...].astype(jnp.float32)
    squared = jnp.sum(values * values, axis=1, keepdims=True)
    unit = (values * lax.rsqrt(squared + epsilon)).astype(jnp.bfloat16)
    slot = owner * capacity + within.astype(jnp.int32)
    spots = groups * capacity
    put = (lax.broadcasted_iota(jnp.int32, (spots, rows), 0) == slot).astype(jnp.bfloat16)
    start = 0
    for ref in send_refs:
        width = ref.shape[1]
        ref[...] = lax.dot_general(
            put,
            unit[:, start : start + width],
            contract_first,
            preferred_element_type=jnp.float32,
        ).astype(jnp.bfloat16)
        start += width
    named = onehot * (cluster_ref[...] + 1).astype(jnp.bfloat16)
    place = lax.broadcasted_iota(jnp.int32, (lanes, rows), 0) == within.astype(jnp.int32)
    ids_ref[...] = (
        lax.dot_general(
            named,
            place.astype(jnp.bfloat16),
            contract_last,
            preferred_element_type=jnp.float32,
        )
        - 1.0
    )


def spread_kernel(ids_ref, out_ref):
    blocks = out_ref.shape[0]
    lane = lax.broadcasted_iota(jnp.int32, (blocks, lanes), 1)
    total = jnp.zeros((blocks, lanes), jnp.float32)
    for i in range(lanes // capacity):
        piece = ids_ref[pl.ds(i, blocks, stride=lanes // capacity), :]
        piece = piece if i == 0 else pltpu.roll(piece, capacity * i, 1)
        total = jnp.where(lane // capacity == i, piece, total)
    out_ref[...] = total


def to_column(row):
    return jnp.transpose(jnp.broadcast_to(row, (lanes, lanes)))


def columns_of(ids, count):
    return jnp.concatenate([to_column(ids[b : b + 1, :]) for b in range(count)], axis=0)


def to_rows(tile):
    blocks = tile.shape[0] // lanes
    return jnp.concatenate(
        [
            jnp.max(jnp.transpose(tile[b * lanes : (b + 1) * lanes, :]), axis=0, keepdims=True)
            for b in range(blocks)
        ],
        axis=0,
    )


wide = 256


def scan_block(lefts, right_of, left_ids, right_ids_ref, at, best, skip_diagonal):
    total = None
    for left, right in zip(lefts, right_of(at)):
        part = lax.dot_general(left, right, contract_last, preferred_element_type=jnp.float32)
        total = part if total is None else total + part
    tops = []
    for half in range(wide // lanes):
        scores = total[:, half * lanes : (half + 1) * lanes]
        ids = right_ids_ref[pl.ds(at * (wide // lanes) + half, 1), :]
        ids = jnp.where(ids < 0, -2.0, ids)
        same = left_ids == ids
        if skip_diagonal:
            row = lax.broadcasted_iota(jnp.int32, scores.shape, 0)
            column = lax.broadcasted_iota(jnp.int32, scores.shape, 1)
            same = same & (row - column != at * wide + half * lanes)
        masked = jnp.where(same, scores, -1.0)
        best = jnp.maximum(best, masked)
        tops.append(jnp.max(masked, axis=0, keepdims=True))
    return best, tops


def own_kernel(parts, *refs):
    own, ids_ref, out_ref, acc = refs[:parts], refs[parts], refs[parts + 1], refs[parts + 2]
    rows = own[0].shape[0]
    columns = columns_of(ids_ref[...], rows // lanes)
    acc[...] = jnp.full(acc.shape, -1.0, jnp.float32)

    def body(at, carry):
        best, _ = scan_block(
            [r[...] for r in own],
            lambda at: [r[pl.ds(at * wide, wide), :] for r in own],
            columns,
            ids_ref,
            at,
            acc[...],
            True,
        )
        acc[...] = best
        return carry

    lax.fori_loop(0, rows // wide, body, 0)
    out_ref[...] = to_rows(acc[...])


def cross_kernel(parts, low_ref, *refs):
    own, after, before = refs[:parts], refs[parts : 2 * parts], refs[2 * parts : 3 * parts]
    ids_ref, after_ids, before_ids, mine_ref, up_ref, down_ref, acc, far, tops, pick = refs[3 * parts :]
    rows = own[0].shape[0]
    half = rows // 2
    low = low_ref[0] == 1
    columns = columns_of(ids_ref[...], rows // lanes)
    acc[...] = jnp.full(acc.shape, -1.0, jnp.float32)
    far[...] = jnp.full(far.shape, -1.0, jnp.float32)
    pick[...] = jnp.where(low, after_ids[...], before_ids[...])
    blocks = rows // lanes
    left_ids = jnp.where(
        low, before_ids[: blocks // 2, :], after_ids[blocks // 2 :, :]
    )
    left_columns = columns_of(left_ids, half // lanes)
    left = [jnp.where(low, b[:half, :], a[half:, :]) for a, b in zip(after, before)]

    def body(at, carry):
        best, found = scan_block(
            [r[...] for r in own],
            lambda at: [r[pl.ds(at * wide, wide), :] for r in after],
            columns,
            after_ids,
            at,
            acc[...],
            False,
        )
        acc[...] = best
        for i, top in enumerate(found):
            up_ref[pl.ds(at * (wide // lanes) + i, 1), :] = top
        spot = pl.ds(at * wide, wide)
        best, found = scan_block(
            left,
            lambda at: [jnp.where(low, a[spot, :], b[spot, :]) for a, b in zip(after, before)],
            left_columns,
            pick,
            at,
            far[...],
            False,
        )
        far[...] = best
        for i, top in enumerate(found):
            tops[pl.ds(at * (wide // lanes) + i, 1), :] = top
        return carry

    lax.fori_loop(0, rows // wide, body, 0)
    mine_ref[...] = to_rows(acc[...])
    side = to_rows(far[...])
    blank = jnp.full(side.shape, -1.0, jnp.float32)
    placed = jnp.where(
        low, jnp.concatenate([side, blank], axis=0), jnp.concatenate([blank, side], axis=0)
    )
    up_ref[...] = jnp.maximum(up_ref[...], jnp.where(low, tops[...], placed))
    down_ref[...] = jnp.where(low, placed, tops[...])


def merge_kernel(a_ref, b_ref, c_ref, d_ref, out_ref):
    best = jnp.maximum(
        jnp.maximum(a_ref[...], b_ref[...]), jnp.maximum(c_ref[...], d_ref[...])
    )
    per = lanes // capacity
    row = lax.broadcasted_iota(jnp.int32, (lanes, lanes), 0)
    lane = lax.broadcasted_iota(jnp.int32, (lanes, lanes), 1)
    for b in range(best.shape[0]):
        tile = jnp.where(row % capacity == lane, to_column(best[b : b + 1, :]), -1.0)
        out_ref[b * per : (b + 1) * per, :] = jnp.max(
            tile.reshape(per, capacity, lanes), axis=1
        )


def fetch_kernel(groups, back_ref, owner_ref, out_ref):
    owner = owner_ref[...]
    rows = owner.shape[1]
    onehot, within = rank_rows(owner, groups)
    rest = back_ref[...]
    found = jnp.zeros((lanes, rows), jnp.float32)
    for _ in range(3):
        piece = rest.astype(jnp.bfloat16)
        rest = rest - piece.astype(jnp.float32)
        found = found + lax.dot_general(
            piece, onehot, (((0,), (0,)), ((), ())), preferred_element_type=jnp.float32
        )
    place = lax.broadcasted_iota(jnp.int32, (lanes, rows), 0) == within.astype(jnp.int32)
    out_ref[...] = jnp.sum(jnp.where(place, found, 0.0), axis=0, keepdims=True)


def shift(values, step):
    count = lax.axis_size("span")
    return lax.ppermute(values, "span", [(i, (i + step) % count) for i in range(count)])


def shards(embeddings, owner, cluster):
    rows = embeddings.shape[0]
    groups = lax.axis_size("ingest")
    spots = groups * capacity
    blocks = spots // lanes
    parts = len(cuts)
    owner = owner.reshape(1, rows)
    cluster = cluster.reshape(1, rows)
    f32 = jnp.float32
    *sends, ids = pl.pallas_call(
        functools.partial(place_kernel, groups),
        out_shape=[jax.ShapeDtypeStruct((spots, w), jnp.bfloat16) for w in cuts]
        + [jax.ShapeDtypeStruct((groups, lanes), f32)],
        compiler_params=params(),
        name="place",
    )(embeddings, owner, cluster)
    own, after, before = [], [], []
    for send in sends:
        got = lax.all_to_all(
            send.reshape(groups, capacity, send.shape[1]),
            "ingest",
            split_axis=0,
            concat_axis=0,
            tiled=True,
        ).reshape(spots, send.shape[1])
        own.append(got)
        before.append(shift(got, 1))
        after.append(shift(got, -1))
    ids, own[-1] = lax.optimization_barrier((ids, own[-1]))
    ids = lax.all_to_all(
        ids.reshape(groups, 1, 1, lanes), "ingest", split_axis=0, concat_axis=0, tiled=True
    ).reshape(groups, lanes)
    ids = pl.pallas_call(
        spread_kernel,
        out_shape=jax.ShapeDtypeStruct((blocks, lanes), f32),
        name="spread",
    )(ids)
    before_ids, after_ids = shift(ids, 1), shift(ids, -1)
    row_shape = jax.ShapeDtypeStruct((blocks, lanes), f32)
    inside = pl.pallas_call(
        functools.partial(own_kernel, parts),
        out_shape=row_shape,
        scratch_shapes=[pltpu.VMEM((spots, lanes), f32)],
        compiler_params=params(),
        name="own",
    )(*own, ids)
    low = (lax.axis_index("span") < lax.axis_size("span") // 2).astype(jnp.int32).reshape(1)
    vmem = pl.BlockSpec(memory_space=pltpu.VMEM)
    mine, up, down = pl.pallas_call(
        functools.partial(cross_kernel, parts),
        out_shape=[row_shape] * 3,
        in_specs=[pl.BlockSpec(memory_space=pltpu.SMEM)] + [vmem] * (3 * parts + 3),
        scratch_shapes=[
            pltpu.VMEM((spots, lanes), f32),
            pltpu.VMEM((spots // 2, lanes), f32),
            pltpu.VMEM((blocks, lanes), f32),
            pltpu.VMEM((blocks, lanes), f32),
        ],
        compiler_params=params(),
        name="cross",
    )(low, *own, *after, *before, ids, after_ids, before_ids)
    from_below, from_above = shift(up, 1), shift(down, -1)
    best = pl.pallas_call(
        merge_kernel,
        out_shape=jax.ShapeDtypeStruct((groups, lanes), f32),
        name="merge",
    )(inside, mine, from_below, from_above)
    back = lax.all_to_all(
        best.reshape(groups, 1, 1, lanes), "ingest", split_axis=0, concat_axis=0, tiled=True
    ).reshape(groups, lanes)
    result = pl.pallas_call(
        functools.partial(fetch_kernel, groups),
        out_shape=jax.ShapeDtypeStruct((1, rows), f32),
        name="fetch",
    )(back, owner)
    return result.reshape(rows)


def solution(mesh):
    placed = (P(("ingest", "span"), None), P(("ingest", "span"), None), P(("ingest", "span")))
    return jax.shard_map(
        shards, mesh=mesh, in_specs=placed, out_specs=P(("ingest", "span")), check_vma=False
    )
```

```python
import functools

import jax
import jax.numpy as jnp
from jax import lax
from jax.experimental import pallas as pl
from jax.experimental.pallas import tpu as pltpu
from jax.sharding import PartitionSpec as P

epsilon = 1e-06
capacity = 16
lanes = 128
wide = 256
cores = 2
places = 4
depth = 8
field = cores * capacity
near_slabs = (0, 1, 7, 2, 6)
far_slabs = (3, 5, 4)
contract_last = (((1,), (1,)), ((), ()))
contract_first = (((1,), (0,)), ((), ()))
everyone = ("ingest", "span")


def params():
    return pltpu.CompilerParams(vmem_limit_bytes=40 * 1024 * 1024)


def device(y, z, core, x):
    return ((y * depth + z) * cores + core) * places + x


def pairs(move):
    found = []
    for y in range(places):
        for z in range(depth):
            for core in range(cores):
                for x in range(places):
                    found.append((device(y, z, core, x), device(*move(y, z, core, x))))
    return found


def along_depth(step):
    return pairs(lambda y, z, core, x: (y, (z + step) % depth, core, x))


def other_core():
    return pairs(lambda y, z, core, x: (y, z, 1 - core, x))


def beside(step):
    return pairs(
        lambda y, z, core, x: (y, z, core, (x + step) % places)
        if core == 0
        else ((y + step) % places, z, core, x)
    )


def line_teams():
    spots = range(places)
    return [[device(i, z, 0, x) for i in spots] for z in range(depth) for x in spots] + [
        [device(y, z, 1, i) for i in spots] for z in range(depth) for y in spots
    ]


def plane_teams():
    spots, levels = range(places), range(depth)
    return [[device(i, z, 0, x) for i in spots for z in levels] for x in spots] + [
        [device(y, z, 1, i) for i in spots for z in levels] for y in spots
    ]


def chunks():
    found = []
    for place in range(places):
        for slab in near_slabs:
            found.append((place, slab))
    for place in range(places):
        for slab in far_slabs:
            found.append((place, slab))
    return found


def rank_rows(owner, groups):
    rows = owner.shape[1]
    belongs = lax.broadcasted_iota(jnp.int32, (groups, rows), 0) == owner
    onehot = belongs.astype(jnp.bfloat16)
    earlier = lax.broadcasted_iota(jnp.int32, (rows, rows), 0) < lax.broadcasted_iota(
        jnp.int32, (rows, rows), 1
    )
    before = lax.dot_general(
        onehot, earlier.astype(jnp.bfloat16), contract_first, preferred_element_type=jnp.float32
    )
    return jnp.sum(jnp.where(belongs, before, 0.0), axis=0, keepdims=True).astype(jnp.int32)


def owned_here(owner, core):
    half = owner.shape[1]
    table = lax.broadcasted_iota(jnp.int32, (places * depth, half), 0)
    return (table == owner // cores) & (owner % cores == core)


def place_kernel(groups, spot_ref, *refs):
    embs, owners, clusters = refs[0:2], refs[2:4], refs[4:6]
    slabs, ids_ref, within_ref = refs[6 : 6 + depth], refs[6 + depth], refs[7 + depth]
    core, level = spot_ref[0], spot_ref[1]
    slots, units, named, spots = [], [], [], []
    for side in range(cores):
        owner = owners[side][...]
        within = rank_rows(owner, groups)
        within_ref[side : side + 1, :] = within
        team = owner // cores
        away = (team % depth - level + depth) % depth
        slot = (away * places + team // depth) * field + side * capacity + within
        slots.append(jnp.where(owner % cores == core, slot, -1))
        values = embs[side][...].astype(jnp.float32)
        squared = jnp.sum(values * values, axis=1, keepdims=True)
        units.append((values * lax.rsqrt(squared + epsilon)).astype(jnp.bfloat16))
        here = owned_here(owner, core).astype(jnp.bfloat16)
        named.append(here * (clusters[side][...] + 1).astype(jnp.bfloat16))
        spots.append(within + side * capacity)
    slot = jnp.concatenate(slots, axis=1)
    unit = jnp.concatenate(units, axis=0)
    rows = slot.shape[1]
    room = depth * places * field
    put = (lax.broadcasted_iota(jnp.int32, (room, rows), 0) == slot).astype(jnp.bfloat16)
    each = places * field
    for start in range(0, unit.shape[1], wide):
        placed = lax.dot_general(
            put,
            unit[:, start : start + wide],
            contract_first,
            preferred_element_type=jnp.float32,
        ).astype(jnp.bfloat16)
        for i, ref in enumerate(slabs):
            ref[:, start : start + wide] = placed[i * each : (i + 1) * each, :]
    lane = lax.broadcasted_iota(jnp.int32, (lanes, rows), 0)
    into = (lane == jnp.concatenate(spots, axis=1)).astype(jnp.bfloat16)
    ids_ref[...] = (
        lax.dot_general(
            jnp.concatenate(named, axis=1),
            into,
            contract_last,
            preferred_element_type=jnp.float32,
        )
        - 1.0
    )


def spread_kernel(spot_ref, ids_ref, out_ref):
    level = spot_ref[1]
    lane = lax.broadcasted_iota(jnp.int32, (1, lanes), 1)
    per = lanes // field
    for i, (place, slab) in enumerate(chunks()):
        source = place * depth + (level - slab + depth) % depth
        piece = ids_ref[pl.ds(source, 1), :]
        if i % per == 0:
            total = piece
        else:
            total = jnp.where(lane // field == i % per, pltpu.roll(piece, field * (i % per), 1), total)
        if i % per == per - 1:
            out_ref[i // per : i // per + 1, :] = total


def to_column(row):
    return jnp.transpose(jnp.broadcast_to(row, (lanes, lanes)))


def columns_of(ids):
    return jnp.concatenate([to_column(ids[b : b + 1, :]) for b in range(ids.shape[0])], axis=0)


def to_rows(tile):
    return jnp.concatenate(
        [
            jnp.max(jnp.transpose(tile[b * lanes : (b + 1) * lanes, :]), axis=0, keepdims=True)
            for b in range(tile.shape[0] // lanes)
        ],
        axis=0,
    )


def block_of(refs, start, count):
    found = []
    for ref in refs:
        low, high = max(start, 0), min(start + count, ref.shape[0])
        if low < high:
            found.append(ref[low:high, :])
        start -= ref.shape[0]
    return found[0] if len(found) == 1 else jnp.concatenate(found, axis=0)


def scan_block(lefts, right, left_ids, right_ids, best, skip):
    parts = [
        lax.dot_general(left, right, contract_last, preferred_element_type=jnp.float32)
        for left in lefts
    ]
    total = parts[0] if len(parts) == 1 else jnp.concatenate(parts, axis=0)
    tops = []
    for half in range(wide // lanes):
        scores = total[:, half * lanes : (half + 1) * lanes]
        ids = right_ids[half : half + 1, :]
        same = left_ids == jnp.where(ids < 0, -2.0, ids)
        if skip is not None:
            row = lax.broadcasted_iota(jnp.int32, scores.shape, 0)
            column = lax.broadcasted_iota(jnp.int32, scores.shape, 1)
            same = same & (row - column != skip + half * lanes)
        masked = jnp.where(same, scores, -1.0)
        best = masked if best is None else jnp.maximum(best, masked)
        tops.append(jnp.max(masked, axis=0, keepdims=True))
    return best, tops


def own_kernel(spot_ref, *refs):
    *own, ids_ref, out_ref = refs
    ids = ids_ref[...]
    rows = ids.shape[0] * lanes
    columns = columns_of(ids)
    lefts = [r[...] for r in own]
    best = None
    per = wide // lanes
    for at in range(rows // wide):
        best, _ = scan_block(
            lefts,
            block_of(own, at * wide, wide),
            columns,
            ids[at * per : (at + 1) * per, :],
            best,
            at * wide,
        )
    out_ref[...] = to_rows(best)


def cross_kernel(sets, spot_ref, *refs):
    own, after, before = refs[:sets], refs[sets : 2 * sets], refs[2 * sets : 3 * sets]
    ids_ref, after_ids_ref, before_ids_ref, inside_ref, out_ref = refs[3 * sets :]
    level, low = spot_ref[1], spot_ref[2] == 1
    ids, after_ids, before_ids = ids_ref[...], after_ids_ref[...], before_ids_ref[...]
    blocks = ids.shape[0]
    rows = blocks * lanes
    half = rows // 2
    columns = columns_of(ids)
    right_ids = jnp.where(low, after_ids, before_ids)
    left_ids = jnp.where(low, before_ids[: blocks // 2, :], after_ids[blocks // 2 :, :])
    left_columns = columns_of(left_ids)
    left = jnp.where(low, block_of(before, 0, half), block_of(after, half, half))
    lefts = [r[...] for r in own]
    per = wide // lanes
    best, far, up, side = None, None, [], []
    for at in range(rows // wide):
        near = block_of(after, at * wide, wide)
        right = jnp.where(low, near, block_of(before, at * wide, wide))
        cut = slice(at * per, (at + 1) * per)
        best, tops = scan_block(lefts, near, columns, after_ids[cut, :], best, None)
        up += tops
        far, tops = scan_block([left], right, left_columns, right_ids[cut, :], far, None)
        side += tops
    up, side = jnp.concatenate(up, axis=0), jnp.concatenate(side, axis=0)
    mine = jnp.maximum(to_rows(best), inside_ref[...])
    found = to_rows(far)
    blank = jnp.full(found.shape, -1.0, jnp.float32)
    placed = jnp.where(
        low, jnp.concatenate([found, blank], axis=0), jnp.concatenate([blank, found], axis=0)
    )
    up = jnp.maximum(up, jnp.where(low, side, placed))
    down = jnp.where(low, placed, side)
    lane = lax.broadcasted_iota(jnp.int32, (blocks, lanes), 1)
    count = lanes // field
    for q in range(count):
        turned = [
            values if (i - q) % count == 0 else pltpu.roll(values, field * ((i - q) % count), 1)
            for i, values in enumerate((mine, up, down))
        ]
        joined = jnp.where(
            lane < field, turned[0], jnp.where(lane < 2 * field, turned[1], turned[2])
        )
        for i, (place, slab) in enumerate(chunks()):
            if i % count == q:
                source = place * depth + (level - slab + depth) % depth
                out_ref[pl.ds(source, 1), :] = joined[i // count : i // count + 1, :]


def fetch_kernel(spot_ref, back_ref, below_ref, above_ref, owner_ref, other_ref, within_ref, out_ref):
    core = spot_ref[0]
    table = jnp.maximum(
        back_ref[...],
        jnp.maximum(
            pltpu.roll(below_ref[...], lanes - field, 1),
            pltpu.roll(above_ref[...], lanes - 2 * field, 1),
        ),
    )
    owners = (owner_ref[...], other_ref[...])
    here = [owned_here(owner, core) for owner in owners]
    onehot = jnp.concatenate(here, axis=1).astype(jnp.bfloat16)
    rows = owners[0].shape[1]
    rest = table
    found = jnp.zeros((lanes, cores * rows), jnp.float32)
    for _ in range(3):
        piece = rest.astype(jnp.bfloat16)
        rest = rest - piece.astype(jnp.float32)
        found = found + lax.dot_general(
            piece, onehot, (((0,), (0,)), ((), ())), preferred_element_type=jnp.float32
        )
    lane = lax.broadcasted_iota(jnp.int32, (lanes, rows), 0)
    for side in range(cores):
        place = lane == within_ref[side : side + 1, :] + side * capacity
        part = found[:, side * rows : (side + 1) * rows]
        picked = jnp.sum(jnp.where(place, part, 0.0), axis=0, keepdims=True)
        mine = owners[side] % cores == core
        out_ref[side : side + 1, :] = jnp.where(mine, picked, -1.0)


def send(values, route):
    return lax.ppermute(values, everyone, route)


def trade(values, teams):
    return lax.all_to_all(
        values, everyone, split_axis=0, concat_axis=0, axis_index_groups=teams, tiled=True
    )


def shards(embeddings, owner, cluster):
    rows, width = embeddings.shape
    groups = lax.axis_size("ingest")
    spots = groups * capacity
    blocks = spots // lanes
    each = places * field
    f32 = jnp.float32
    at, x = lax.axis_index("ingest"), lax.axis_index("span")
    core, level, y = at % cores, at // cores % depth, at // (cores * depth)
    low = jnp.where(core == 0, x, y) < places // 2
    spot = jnp.stack([core, level, low.astype(jnp.int32)]).astype(jnp.int32)
    smem, vmem = pl.BlockSpec(memory_space=pltpu.SMEM), pl.BlockSpec(memory_space=pltpu.VMEM)

    def call(kernel, out_shape, name, *args):
        return pl.pallas_call(
            kernel,
            out_shape=out_shape,
            in_specs=[smem] + [vmem] * len(args),
            compiler_params=params(),
            name=name,
        )(spot, *args)

    swap = other_core()
    owner = owner.reshape(1, rows)
    cluster = cluster.reshape(1, rows)
    others = send(owner, swap)
    other_cluster = send(cluster, swap)
    other_rows = send(embeddings, swap)
    *slabs, ids, within = call(
        functools.partial(place_kernel, groups),
        [jax.ShapeDtypeStruct((each, width), jnp.bfloat16)] * depth
        + [
            jax.ShapeDtypeStruct((places * depth, lanes), f32),
            jax.ShapeDtypeStruct((cores, rows), jnp.int32),
        ],
        "place",
        embeddings,
        other_rows,
        owner,
        others,
        cluster,
        other_cluster,
    )
    for slab in near_slabs[1:] + far_slabs:
        slabs[slab] = send(slabs[slab], along_depth(slab))
    teams = plane_teams()
    ids = trade(ids.reshape(places * depth, 1, 1, lanes), teams).reshape(places * depth, lanes)
    ids = call(spread_kernel, jax.ShapeDtypeStruct((blocks, lanes), f32), "spread", ids)
    before_ids, after_ids = send(ids, beside(1)), send(ids, beside(-1))
    own, after, before = [], [], []
    for chosen in (near_slabs, far_slabs):
        group = jnp.concatenate(
            [slabs[s].reshape(places, field, width) for s in chosen], axis=1
        )
        got = trade(group, line_teams()).reshape(len(chosen) * each, width)
        own.append(got)
        before.append(send(got, beside(1)))
        after.append(send(got, beside(-1)))
    inside = call(own_kernel, jax.ShapeDtypeStruct((blocks, lanes), f32), "own", *own, ids)
    best = call(
        functools.partial(cross_kernel, len(own)),
        jax.ShapeDtypeStruct((places * depth, lanes), f32),
        "cross",
        *own,
        *after,
        *before,
        ids,
        after_ids,
        before_ids,
        inside,
    )
    back = trade(best.reshape(places * depth, 1, 1, lanes), teams).reshape(places * depth, lanes)
    below, above = send(back, beside(1)), send(back, beside(-1))
    found = call(
        fetch_kernel,
        jax.ShapeDtypeStruct((cores, rows), f32),
        "fetch",
        back,
        below,
        above,
        owner,
        others,
        within,
    )
    return jnp.maximum(found[0], send(found[1], swap))


def solution(mesh):
    placed = (P(("ingest", "span"), None), P(("ingest", "span"), None), P(("ingest", "span")))
    return jax.shard_map(
        shards, mesh=mesh, in_specs=placed, out_specs=P(("ingest", "span")), check_vma=False
    )
```

```python
import functools

import jax
import jax.numpy as jnp
from jax import lax
from jax.experimental import pallas as pl
from jax.experimental.pallas import tpu as pltpu
from jax.sharding import PartitionSpec as P

epsilon = 1e-06
capacity = 16
lanes = 128
wide = 256
cores = 2
places = 4
depth = 8
field = cores * capacity
cuts = (1024,)
contract_last = (((1,), (1,)), ((), ()))
contract_first = (((1,), (0,)), ((), ()))
everyone = ("ingest", "span")


def params():
    return pltpu.CompilerParams(vmem_limit_bytes=40 * 1024 * 1024)


def device(y, z, core, x):
    return ((y * depth + z) * cores + core) * places + x


def pairs(move):
    found = []
    for y in range(places):
        for z in range(depth):
            for core in range(cores):
                for x in range(places):
                    found.append((device(y, z, core, x), device(*move(y, z, core, x))))
    return found


def other_core():
    return pairs(lambda y, z, core, x: (y, z, 1 - core, x))


def beside(step, swapped=False):
    def move(y, z, core, x):
        found = 1 - core if swapped else core
        if core == 0:
            return (y, z, found, (x + step) % places)
        return ((y + step) % places, z, found, x)

    return pairs(move)


def plane_teams():
    spots, levels = range(places), range(depth)
    return [[device(i, z, 0, x) for i in spots for z in levels] for x in spots] + [
        [device(y, z, 1, i) for i in spots for z in levels] for y in spots
    ]


def rank_rows(owner, groups):
    rows = owner.shape[1]
    belongs = lax.broadcasted_iota(jnp.int32, (groups, rows), 0) == owner
    onehot = belongs.astype(jnp.bfloat16)
    earlier = lax.broadcasted_iota(jnp.int32, (rows, rows), 0) < lax.broadcasted_iota(
        jnp.int32, (rows, rows), 1
    )
    before = lax.dot_general(
        onehot, earlier.astype(jnp.bfloat16), contract_first, preferred_element_type=jnp.float32
    )
    return jnp.sum(jnp.where(belongs, before, 0.0), axis=0, keepdims=True).astype(jnp.int32)


def owned_here(owner, core):
    half = owner.shape[1]
    table = lax.broadcasted_iota(jnp.int32, (places * depth, half), 0)
    return (table == owner // cores) & (owner % cores == core)


def place_kernel(groups, spot_ref, *refs):
    embs, owners, clusters = refs[0:2], refs[2:4], refs[4:6]
    *sends, ids_ref, within_ref = refs[6:]
    core = spot_ref[0]
    slots, units, named, spots = [], [], [], []
    for side in range(cores):
        owner = owners[side][...]
        within = rank_rows(owner, groups)
        if side == 0:
            within_ref[...] = within
        slot = owner // cores * field + side * capacity + within
        slots.append(jnp.where(owner % cores == core, slot, -1))
        values = embs[side][...].astype(jnp.float32)
        squared = jnp.sum(values * values, axis=1, keepdims=True)
        units.append((values * lax.rsqrt(squared + epsilon)).astype(jnp.bfloat16))
        here = owned_here(owner, core).astype(jnp.bfloat16)
        named.append(here * (clusters[side][...] + 1).astype(jnp.bfloat16))
        spots.append(within + side * capacity)
    slot = jnp.concatenate(slots, axis=1)
    unit = jnp.concatenate(units, axis=0)
    rows = slot.shape[1]
    room = sends[0].shape[0]
    put = (lax.broadcasted_iota(jnp.int32, (room, rows), 0) == slot).astype(jnp.bfloat16)
    base = 0
    for ref in sends:
        for start in range(0, ref.shape[1], wide):
            ref[:, start : start + wide] = lax.dot_general(
                put,
                unit[:, base + start : base + start + wide],
                contract_first,
                preferred_element_type=jnp.float32,
            ).astype(jnp.bfloat16)
        base += ref.shape[1]
    lane = lax.broadcasted_iota(jnp.int32, (lanes, rows), 0)
    into = (lane == jnp.concatenate(spots, axis=1)).astype(jnp.bfloat16)
    ids_ref[...] = (
        lax.dot_general(
            jnp.concatenate(named, axis=1),
            into,
            contract_last,
            preferred_element_type=jnp.float32,
        )
        - 1.0
    )


def spread_kernel(ids_ref, out_ref):
    blocks, count = out_ref.shape[0], lanes // field
    lane = lax.broadcasted_iota(jnp.int32, (blocks, lanes), 1)
    total = ids_ref[pl.ds(0, blocks, stride=count), :]
    for q in range(1, count):
        piece = pltpu.roll(ids_ref[pl.ds(q, blocks, stride=count), :], field * q, 1)
        total = jnp.where(lane // field == q, piece, total)
    out_ref[...] = total


def to_column(row):
    return jnp.transpose(jnp.broadcast_to(row, (lanes, lanes)))


def columns_of(ids):
    return jnp.concatenate([to_column(ids[b : b + 1, :]) for b in range(ids.shape[0])], axis=0)


def to_rows(tile):
    return jnp.concatenate(
        [
            jnp.max(jnp.transpose(tile[b * lanes : (b + 1) * lanes, :]), axis=0, keepdims=True)
            for b in range(tile.shape[0] // lanes)
        ],
        axis=0,
    )


def scan_block(lefts, rights, left_ids, right_ids, best, skip):
    total = None
    for left, right in zip(lefts, rights):
        part = lax.dot_general(left, right, contract_last, preferred_element_type=jnp.float32)
        total = part if total is None else total + part
    tops = []
    for half in range(wide // lanes):
        scores = total[:, half * lanes : (half + 1) * lanes]
        ids = right_ids[half : half + 1, :]
        same = left_ids == jnp.where(ids < 0, -2.0, ids)
        if skip is not None:
            row = lax.broadcasted_iota(jnp.int32, scores.shape, 0)
            column = lax.broadcasted_iota(jnp.int32, scores.shape, 1)
            same = same & (row - column != skip + half * lanes)
        masked = jnp.where(same, scores, -1.0)
        best = masked if best is None else jnp.maximum(best, masked)
        tops.append(jnp.max(masked, axis=0, keepdims=True))
    return best, tops


def own_kernel(*refs):
    *own, ids_ref, out_ref = refs
    ids = ids_ref[...]
    rows = ids.shape[0] * lanes
    columns = columns_of(ids)
    lefts = [r[...] for r in own]
    best = None
    per = wide // lanes
    for at in range(rows // wide):
        best, _ = scan_block(
            lefts,
            [r[at * wide : (at + 1) * wide, :] for r in own],
            columns,
            ids[at * per : (at + 1) * per, :],
            best,
            at * wide,
        )
    out_ref[...] = to_rows(best)


def cross_kernel(parts, spot_ref, *refs):
    own, after, before = refs[:parts], refs[parts : 2 * parts], refs[2 * parts : 3 * parts]
    ids_ref, after_ids_ref, before_ids_ref, inside_ref, out_ref = refs[3 * parts :]
    low = spot_ref[1] == 1
    ids, after_ids, before_ids = ids_ref[...], after_ids_ref[...], before_ids_ref[...]
    blocks = ids.shape[0]
    rows = blocks * lanes
    half = rows // 2
    columns = columns_of(ids)
    right_ids = jnp.where(low, after_ids, before_ids)
    left_ids = jnp.where(low, before_ids[: blocks // 2, :], after_ids[blocks // 2 :, :])
    left_columns = columns_of(left_ids)
    left = [jnp.where(low, b[:half, :], a[half:, :]) for a, b in zip(after, before)]
    lefts = [r[...] for r in own]
    per = wide // lanes
    best, far, up, side = None, None, [], []
    for at in range(rows // wide):
        spot = slice(at * wide, (at + 1) * wide)
        near = [a[spot, :] for a in after]
        right = [jnp.where(low, a, b[spot, :]) for a, b in zip(near, before)]
        cut = slice(at * per, (at + 1) * per)
        best, tops = scan_block(lefts, near, columns, after_ids[cut, :], best, None)
        up += tops
        far, tops = scan_block(left, right, left_columns, right_ids[cut, :], far, None)
        side += tops
    up, side = jnp.concatenate(up, axis=0), jnp.concatenate(side, axis=0)
    mine = jnp.maximum(to_rows(best), inside_ref[...])
    found = to_rows(far)
    blank = jnp.full(found.shape, -1.0, jnp.float32)
    placed = jnp.where(
        low, jnp.concatenate([found, blank], axis=0), jnp.concatenate([blank, found], axis=0)
    )
    up = jnp.maximum(up, jnp.where(low, side, placed))
    down = jnp.where(low, placed, side)
    lane = lax.broadcasted_iota(jnp.int32, (blocks, lanes), 1)
    count = lanes // field
    for q in range(count):
        turned = [
            values if (i - q) % count == 0 else pltpu.roll(values, field * ((i - q) % count), 1)
            for i, values in enumerate((mine, up, down))
        ]
        joined = jnp.where(
            lane < field, turned[0], jnp.where(lane < 2 * field, turned[1], turned[2])
        )
        out_ref[pl.ds(q, blocks, stride=count), :] = joined


def fetch_kernel(spot_ref, *refs):
    *tables, owner_ref, within_ref, out_ref = refs
    core = spot_ref[0]
    joined = []
    for side in range(cores):
        own, below, above = tables[3 * side : 3 * side + 3]
        joined.append(
            jnp.maximum(
                own[...],
                jnp.maximum(
                    pltpu.roll(below[...], lanes - field, 1),
                    pltpu.roll(above[...], lanes - 2 * field, 1),
                ),
            )
        )
    spread = lax.broadcasted_iota(jnp.int32, joined[0].shape, 1)
    rest = jnp.where(spread < capacity, joined[0], joined[1])
    owner = owner_ref[...]
    rows = owner.shape[1]
    team = lax.broadcasted_iota(jnp.int32, (places * depth, rows), 0)
    onehot = (team == owner // cores).astype(jnp.bfloat16)
    found = jnp.zeros((lanes, rows), jnp.float32)
    for _ in range(3):
        piece = rest.astype(jnp.bfloat16)
        rest = rest - piece.astype(jnp.float32)
        found = found + lax.dot_general(
            piece, onehot, (((0,), (0,)), ((), ())), preferred_element_type=jnp.float32
        )
    lane = lax.broadcasted_iota(jnp.int32, (lanes, rows), 0)
    within = within_ref[...] + jnp.where(owner % cores == core, 0, capacity)
    out_ref[...] = jnp.sum(jnp.where(lane == within, found, 0.0), axis=0, keepdims=True)


def send(values, route):
    return lax.ppermute(values, everyone, route)


def trade(values, teams):
    return lax.all_to_all(
        values, everyone, split_axis=0, concat_axis=0, axis_index_groups=teams, tiled=True
    )


def shards(embeddings, owner, cluster):
    rows, width = embeddings.shape
    groups = lax.axis_size("ingest")
    spots = groups * capacity
    blocks = spots // lanes
    each = places * depth
    f32 = jnp.float32
    at, x = lax.axis_index("ingest"), lax.axis_index("span")
    core, y = at % cores, at // (cores * depth)
    low = jnp.where(core == 0, x, y) < places // 2
    spot = jnp.stack([core, low.astype(jnp.int32)]).astype(jnp.int32)
    smem, vmem = pl.BlockSpec(memory_space=pltpu.SMEM), pl.BlockSpec(memory_space=pltpu.VMEM)

    def call(kernel, out_shape, name, *args):
        return pl.pallas_call(
            kernel,
            out_shape=out_shape,
            in_specs=[smem if a is spot else vmem for a in args],
            compiler_params=params(),
            name=name,
        )(*args)

    swap = other_core()
    owner = owner.reshape(1, rows)
    cluster = cluster.reshape(1, rows)
    others = send(owner, swap)
    other_cluster = send(cluster, swap)
    other_rows = send(embeddings, swap)
    *parts, ids, within = call(
        functools.partial(place_kernel, groups),
        [jax.ShapeDtypeStruct((spots, w), jnp.bfloat16) for w in cuts]
        + [
            jax.ShapeDtypeStruct((each, lanes), f32),
            jax.ShapeDtypeStruct((1, rows), jnp.int32),
        ],
        "place",
        spot,
        embeddings,
        other_rows,
        owner,
        others,
        cluster,
        other_cluster,
    )
    teams = plane_teams()
    own, after, before = [], [], []
    for part in parts:
        got = trade(part.reshape(each, field, part.shape[1]), teams).reshape(part.shape)
        own.append(got)
        before.append(send(got, beside(1)))
        after.append(send(got, beside(-1)))
    ids, own[-1] = lax.optimization_barrier((ids, own[-1]))
    ids = trade(ids.reshape(each, 1, 1, lanes), teams).reshape(each, lanes)
    ids = call(spread_kernel, jax.ShapeDtypeStruct((blocks, lanes), f32), "spread", ids)
    before_ids, after_ids = send(ids, beside(1)), send(ids, beside(-1))
    inside = call(own_kernel, jax.ShapeDtypeStruct((blocks, lanes), f32), "own", *own, ids)
    best = call(
        functools.partial(cross_kernel, len(own)),
        jax.ShapeDtypeStruct((each, lanes), f32),
        "cross",
        spot,
        *own,
        *after,
        *before,
        ids,
        after_ids,
        before_ids,
        inside,
    )
    back = trade(best.reshape(each, 1, 1, lanes), teams).reshape(each, lanes)
    tables = [back] + [send(back, beside(step)) for step in (1, -1)]
    tables += [send(back, swap)] + [send(back, beside(step, True)) for step in (1, -1)]
    result = call(
        fetch_kernel, jax.ShapeDtypeStruct((1, rows), f32), "fetch", spot, *tables, owner, within
    )
    return result.reshape(rows)


def solution(mesh):
    placed = (P(("ingest", "span"), None), P(("ingest", "span"), None), P(("ingest", "span")))
    return jax.shard_map(
        shards, mesh=mesh, in_specs=placed, out_specs=P(("ingest", "span")), check_vma=False
    )
```

```python
import functools

import jax
import jax.numpy as jnp
from jax import lax
from jax.experimental import pallas as pl
from jax.experimental.pallas import tpu as pltpu
from jax.sharding import PartitionSpec as P

epsilon = 1e-06
capacity = 16
lanes = 128
wide = 256
cores = 2
places = 4
depth = 8
field = cores * capacity
tail = 128
note = 8
labels = 64
contract_last = (((1,), (1,)), ((), ()))
contract_first = (((1,), (0,)), ((), ()))
everyone = ("ingest", "span")


def params():
    return pltpu.CompilerParams(vmem_limit_bytes=40 * 1024 * 1024)


def device(y, z, core, x):
    return ((y * depth + z) * cores + core) * places + x


def pairs(move):
    found = []
    for y in range(places):
        for z in range(depth):
            for core in range(cores):
                for x in range(places):
                    found.append((device(y, z, core, x), device(*move(y, z, core, x))))
    return found


def other_core():
    return pairs(lambda y, z, core, x: (y, z, 1 - core, x))


def beside(step):
    return pairs(
        lambda y, z, core, x: (y, z, core, (x + step) % places)
        if core == 0
        else ((y + step) % places, z, core, x)
    )


def plane_teams():
    spots, levels = range(places), range(depth)
    return [[device(i, z, 0, x) for i in spots for z in levels] for x in spots] + [
        [device(y, z, 1, i) for i in spots for z in levels] for y in spots
    ]


def rank_rows(owner, groups):
    rows = owner.shape[1]
    belongs = lax.broadcasted_iota(jnp.int32, (groups, rows), 0) == owner
    onehot = belongs.astype(jnp.bfloat16)
    earlier = lax.broadcasted_iota(jnp.int32, (rows, rows), 0) < lax.broadcasted_iota(
        jnp.int32, (rows, rows), 1
    )
    before = lax.dot_general(
        onehot, earlier.astype(jnp.bfloat16), contract_first, preferred_element_type=jnp.float32
    )
    return jnp.sum(jnp.where(belongs, before, 0.0), axis=0, keepdims=True).astype(jnp.int32)


def put_rows(groups, side, spot_ref, emb_ref, name_ref):
    core = spot_ref[0]
    owner = name_ref[...] // labels
    rows = owner.shape[1]
    within = rank_rows(owner, groups)
    slot = jnp.where(owner % cores == core, owner // cores * capacity + within, -1)
    room = groups // cores * capacity
    put = (lax.broadcasted_iota(jnp.int32, (room, rows), 0) == slot).astype(jnp.bfloat16)
    values = emb_ref[...].astype(jnp.float32)
    squared = jnp.sum(values * values, axis=1, keepdims=True)
    unit = (values * lax.rsqrt(squared + epsilon)).astype(jnp.bfloat16)

    def placed(start, width):
        return lax.dot_general(
            put,
            unit[:, start : start + width],
            contract_first,
            preferred_element_type=jnp.float32,
        ).astype(jnp.bfloat16)

    team = lax.broadcasted_iota(jnp.int32, (groups // cores, rows), 0)
    here = (team == owner // cores) & (owner % cores == core)
    named = here.astype(jnp.bfloat16) * (name_ref[...] % labels + 1).astype(jnp.bfloat16)
    lane = lax.broadcasted_iota(jnp.int32, (lanes, rows), 0)
    into = (lane == within + side * capacity).astype(jnp.bfloat16)
    ids = lax.dot_general(named, into, contract_last, preferred_element_type=jnp.float32)
    return placed, ids, within


def place_kernel(groups, spot_ref, emb_ref, name_ref, main_ref, tail_ref, ids_ref, within_ref):
    placed, ids, within = put_rows(groups, 0, spot_ref, emb_ref, name_ref)
    width = main_ref.shape[1]
    for start in range(0, width, wide):
        size = min(wide, width - start)
        main_ref[:, start : start + size] = placed(start, size)
    tail_ref[...] = placed(width, tail)
    ids_ref[...] = ids
    within_ref[...] = within


def pair_kernel(
    groups, spot_ref, emb_ref, name_ref, first_ref, last_ref, ids_ref, main_ref, tail_ref
):
    placed, ids, _ = put_rows(groups, 1, spot_ref, emb_ref, name_ref)
    teams, _, width = main_ref.shape
    main_ref[:, :capacity, :] = first_ref[...].reshape(teams, capacity, width)
    tail_ref[:, :capacity, :] = last_ref[...].reshape(teams, capacity, tail)
    for start in range(0, width, wide):
        size = min(wide, width - start)
        main_ref[:, capacity:field, start : start + size] = placed(start, size).reshape(
            teams, capacity, size
        )
    tail_ref[:, capacity:field, :] = placed(width, tail).reshape(teams, capacity, tail)
    ids = (ids + ids_ref[...] - 1.0).astype(jnp.bfloat16)
    tail_ref[:, field:, :] = jnp.broadcast_to(ids[:, None, :], (teams, note, lanes))


def read_ids(ref, hold):
    count = lanes // field
    blocks = ref.shape[0] // count
    hold[...] = jnp.max(ref[:, field:, :].astype(jnp.float32), axis=1)
    lane = lax.broadcasted_iota(jnp.int32, (blocks, lanes), 1)
    total = hold[pl.ds(0, blocks, stride=count), :]
    for q in range(1, count):
        piece = pltpu.roll(hold[pl.ds(q, blocks, stride=count), :], field * q, 1)
        total = jnp.where(lane // field == q, piece, total)
    return total


def features(main, last, start, count):
    rest = last[start // field : (start + count) // field, :field, :].reshape(count, tail)
    return jnp.concatenate([main[start : start + count, :], rest], axis=1)


def to_column(row):
    return jnp.transpose(jnp.broadcast_to(row, (lanes, lanes)))


def columns_of(ids):
    return jnp.concatenate([to_column(ids[b : b + 1, :]) for b in range(ids.shape[0])], axis=0)


def to_rows(tile):
    return jnp.concatenate(
        [
            jnp.max(jnp.transpose(tile[b * lanes : (b + 1) * lanes, :]), axis=0, keepdims=True)
            for b in range(tile.shape[0] // lanes)
        ],
        axis=0,
    )


def scan_block(left, right, left_ids, right_ids, best, skip):
    total = lax.dot_general(left, right, contract_last, preferred_element_type=jnp.float32)
    tops = []
    for half in range(wide // lanes):
        scores = total[:, half * lanes : (half + 1) * lanes]
        ids = right_ids[half : half + 1, :]
        same = left_ids == jnp.where(ids < 0, -2.0, ids)
        if skip is not None:
            row = lax.broadcasted_iota(jnp.int32, scores.shape, 0)
            column = lax.broadcasted_iota(jnp.int32, scores.shape, 1)
            same = same & (row - column != skip + half * lanes)
        masked = jnp.where(same, scores, -1.0)
        best = masked if best is None else jnp.maximum(best, masked)
        tops.append(jnp.max(masked, axis=0, keepdims=True))
    return best, tops


def own_kernel(main, last, out_ref, ids_ref, hold):
    ids = read_ids(last, hold)
    ids_ref[...] = ids
    rows = main.shape[0]
    columns = columns_of(ids)
    left = features(main, last, 0, rows)
    best = None
    per = wide // lanes
    for at in range(rows // wide):
        best, _ = scan_block(
            left,
            features(main, last, at * wide, wide),
            columns,
            ids[at * per : (at + 1) * per, :],
            best,
            at * wide,
        )
    out_ref[...] = to_rows(best)


def cross_kernel(
    spot_ref,
    main,
    last,
    after,
    after_last,
    before,
    before_last,
    inside_ref,
    ids_ref,
    out_ref,
    hold,
    table,
):
    low = spot_ref[1] == 1
    ids, after_ids, before_ids = (
        ids_ref[...],
        read_ids(after_last, hold.at[0]),
        read_ids(before_last, hold.at[1]),
    )
    blocks = ids.shape[0]
    rows = blocks * lanes
    half = rows // 2
    columns = columns_of(ids)
    right_ids = jnp.where(low, after_ids, before_ids)
    left_ids = jnp.where(low, before_ids[: blocks // 2, :], after_ids[blocks // 2 :, :])
    left_columns = columns_of(left_ids)
    side_left = jnp.where(
        low,
        features(before, before_last, 0, half),
        features(after, after_last, half, half),
    )
    left = features(main, last, 0, rows)
    per = wide // lanes
    best, far, up, side = None, None, [], []
    for at in range(rows // wide):
        near = features(after, after_last, at * wide, wide)
        right = jnp.where(low, near, features(before, before_last, at * wide, wide))
        cut = slice(at * per, (at + 1) * per)
        best, tops = scan_block(left, near, columns, after_ids[cut, :], best, None)
        up += tops
        far, tops = scan_block(side_left, right, left_columns, right_ids[cut, :], far, None)
        side += tops
    up, side = jnp.concatenate(up, axis=0), jnp.concatenate(side, axis=0)
    mine = jnp.maximum(to_rows(best), inside_ref[...])
    found = to_rows(far)
    blank = jnp.full(found.shape, -1.0, jnp.float32)
    placed = jnp.where(
        low, jnp.concatenate([found, blank], axis=0), jnp.concatenate([blank, found], axis=0)
    )
    up = jnp.maximum(up, jnp.where(low, side, placed))
    down = jnp.where(low, placed, side)
    count = lanes // field
    steps = (0, 1, places - 1)
    for step, values in enumerate((mine, up, down)):
        for q in range(count):
            turned = values if q == 0 else pltpu.roll(values, lanes - field * q, 1)
            table[step, pl.ds(q, blocks, stride=count), :] = turned
    core, x, y = spot_ref[0], spot_ref[2], spot_ref[3]
    each = places * depth
    across = cores * places

    def found(step, other):
        values = table[step]
        return jnp.where(other == core, values, pltpu.roll(values, lanes - capacity, 1))

    @pl.when(core == 0)
    def _():
        for step, move in enumerate(steps):
            for other in range(cores):
                start = other * places + lax.rem(x + move, places)
                out_ref[pl.ds(start, each, stride=across), :] = found(step, other)

    @pl.when(core == 1)
    def _():
        for step, move in enumerate(steps):
            row = lax.rem(y + move, places) * (depth * across)
            for other in range(cores):
                values = found(step, other)
                for place in range(places):
                    start = row + other * places + place
                    out_ref[pl.ds(start, depth, stride=across), :] = values[
                        place * depth : (place + 1) * depth, :
                    ]


def fetch_kernel(spot_ref, back_ref, name_ref, within_ref, out_ref):
    x, y = spot_ref[2], spot_ref[3]
    each = places * depth
    across = cores * places
    even, odd = None, []
    for move in (0, 1, places - 1):
        rows = back_ref[pl.ds(lax.rem(x + move, places), each, stride=across), :]
        even = rows if even is None else jnp.maximum(even, rows)
    for place in range(places):
        total = None
        for move in (0, 1, places - 1):
            start = lax.rem(y + move, places) * (depth * across) + places + place
            rows = back_ref[pl.ds(start, depth, stride=across), :]
            total = rows if total is None else jnp.maximum(total, rows)
        odd.append(total)
    odd = pltpu.roll(jnp.concatenate(odd, axis=0), capacity, 1)
    rest = jnp.where(lax.broadcasted_iota(jnp.int32, even.shape, 1) < capacity, even, odd)
    rest = jnp.where(lax.broadcasted_iota(jnp.int32, even.shape, 1) < field, rest, 0.0)
    owner = name_ref[...] // labels
    rows = owner.shape[1]
    team = lax.broadcasted_iota(jnp.int32, (places * depth, rows), 0)
    onehot = (team == owner // cores).astype(jnp.bfloat16)
    found = jnp.zeros((lanes, rows), jnp.float32)
    for _ in range(3):
        piece = rest.astype(jnp.bfloat16)
        rest = rest - piece.astype(jnp.float32)
        found = found + lax.dot_general(
            piece, onehot, (((0,), (0,)), ((), ())), preferred_element_type=jnp.float32
        )
    lane = lax.broadcasted_iota(jnp.int32, (lanes, rows), 0)
    within = within_ref[...] + owner % cores * capacity
    out_ref[...] = jnp.sum(jnp.where(lane == within, found, 0.0), axis=0, keepdims=True)


def send(values, route):
    return lax.ppermute(values, everyone, route)


def trade(values, teams):
    return lax.all_to_all(
        values, everyone, split_axis=0, concat_axis=0, axis_index_groups=teams, tiled=True
    )


def shards(embeddings, owner, cluster):
    rows, width = embeddings.shape
    groups = lax.axis_size("ingest")
    spots = groups * capacity
    blocks = spots // lanes
    each = places * depth
    f32 = jnp.float32
    at, x = lax.axis_index("ingest"), lax.axis_index("span")
    core, y = at % cores, at // (cores * depth)
    low = jnp.where(core == 0, x, y) < places // 2
    spot = jnp.stack([core, low.astype(jnp.int32), x, y]).astype(jnp.int32)
    smem, vmem = pl.BlockSpec(memory_space=pltpu.SMEM), pl.BlockSpec(memory_space=pltpu.VMEM)

    def call(kernel, out_shape, name, *args, scratch=()):
        return pl.pallas_call(
            kernel,
            out_shape=out_shape,
            in_specs=[smem if a is spot else vmem for a in args],
            scratch_shapes=scratch,
            compiler_params=params(),
            name=name,
        )(*args)

    def array(*shape, dtype=jnp.bfloat16):
        return jax.ShapeDtypeStruct(shape, dtype)

    swap = other_core()
    names = owner.reshape(1, rows) * labels + cluster.reshape(1, rows)
    other_rows = send(embeddings, swap)
    other_names = send(names, swap)
    first, last, ids, within = call(
        functools.partial(place_kernel, groups),
        [
            array(spots // cores, width - tail),
            array(spots // cores, tail),
            array(each, lanes, dtype=f32),
            array(1, rows, dtype=jnp.int32),
        ],
        "place",
        spot,
        embeddings,
        names,
    )
    parts = call(
        functools.partial(pair_kernel, groups),
        [array(each, field, width - tail), array(each, field + note, tail)],
        "pair",
        spot,
        other_rows,
        other_names,
        first,
        last,
        ids,
    )
    teams = plane_teams()
    own, after, before = [], [], []
    for part in parts:
        got = trade(part, teams)
        if not own:
            got = got.reshape(spots, width - tail)
        own.append(got)
        before.append(send(got, beside(1)))
        after.append(send(got, beside(-1)))
    inside, ids = call(
        own_kernel,
        [array(blocks, lanes, dtype=f32)] * 2,
        "own",
        *own,
        scratch=[pltpu.VMEM((each, lanes), f32)],
    )
    count = groups * places
    best = call(
        cross_kernel,
        array(count, lanes, dtype=f32),
        "cross",
        spot,
        *own,
        *after,
        *before,
        inside,
        ids,
        scratch=[pltpu.VMEM((2, each, lanes), f32), pltpu.VMEM((3, each, lanes), f32)],
    )
    back = lax.all_to_all(
        best.reshape(count, 1, 1, lanes), everyone, split_axis=0, concat_axis=0, tiled=True
    ).reshape(count, lanes)
    result = call(fetch_kernel, array(1, rows, dtype=f32), "fetch", spot, back, names, within)
    return result.reshape(rows)


def solution(mesh):
    placed = (P(("ingest", "span"), None), P(("ingest", "span"), None), P(("ingest", "span")))
    return jax.shard_map(
        shards, mesh=mesh, in_specs=placed, out_specs=P(("ingest", "span")), check_vma=False
    )
```

```python
import functools

import jax
import jax.numpy as jnp
from jax import lax
from jax.experimental import pallas as pl
from jax.experimental.pallas import tpu as pltpu
from jax.sharding import PartitionSpec as P

epsilon = 1e-06
capacity = 16
lanes = 128
wide = 256
cores = 2
places = 4
depth = 8
field = cores * capacity
tail = 128
note = 8
labels = 64
contract_last = (((1,), (1,)), ((), ()))
contract_first = (((1,), (0,)), ((), ()))
everyone = ("ingest", "span")


def params():
    return pltpu.CompilerParams(vmem_limit_bytes=40 * 1024 * 1024)


def device(y, z, core, x):
    return ((y * depth + z) * cores + core) * places + x


def pairs(move):
    found = []
    for y in range(places):
        for z in range(depth):
            for core in range(cores):
                for x in range(places):
                    found.append((device(y, z, core, x), device(*move(y, z, core, x))))
    return found


def other_core():
    return pairs(lambda y, z, core, x: (y, z, 1 - core, x))


def beside(step):
    return pairs(
        lambda y, z, core, x: (y, z, core, (x + step) % places)
        if core == 0
        else ((y + step) % places, z, core, x)
    )


def plane_teams():
    spots, levels = range(places), range(depth)
    return [[device(i, z, 0, x) for i in spots for z in levels] for x in spots] + [
        [device(y, z, 1, i) for i in spots for z in levels] for y in spots
    ]


def rank_rows(owner, groups):
    rows = owner.shape[1]
    belongs = lax.broadcasted_iota(jnp.int32, (groups, rows), 0) == owner
    onehot = belongs.astype(jnp.bfloat16)
    earlier = lax.broadcasted_iota(jnp.int32, (rows, rows), 0) < lax.broadcasted_iota(
        jnp.int32, (rows, rows), 1
    )
    before = lax.dot_general(
        onehot, earlier.astype(jnp.bfloat16), contract_first, preferred_element_type=jnp.float32
    )
    return jnp.sum(jnp.where(belongs, before, 0.0), axis=0, keepdims=True).astype(jnp.int32)


def put_rows(groups, side, spot_ref, emb_ref, name_ref):
    core = spot_ref[0]
    owner = name_ref[...] // labels
    rows = owner.shape[1]
    within = rank_rows(owner, groups)
    slot = jnp.where(owner % cores == core, owner // cores * capacity + within, -1)
    room = groups // cores * capacity
    put = (lax.broadcasted_iota(jnp.int32, (room, rows), 0) == slot).astype(jnp.bfloat16)
    values = emb_ref[...].astype(jnp.float32)
    squared = jnp.sum(values * values, axis=1, keepdims=True)
    unit = (values * lax.rsqrt(squared + epsilon)).astype(jnp.bfloat16)

    def placed(start, width):
        return lax.dot_general(
            put,
            unit[:, start : start + width],
            contract_first,
            preferred_element_type=jnp.float32,
        ).astype(jnp.bfloat16)

    team = lax.broadcasted_iota(jnp.int32, (groups // cores, rows), 0)
    here = (team == owner // cores) & (owner % cores == core)
    named = here.astype(jnp.bfloat16) * (name_ref[...] % labels + 1).astype(jnp.bfloat16)
    lane = lax.broadcasted_iota(jnp.int32, (lanes, rows), 0)
    into = (lane == within + side * capacity).astype(jnp.bfloat16)
    ids = lax.dot_general(named, into, contract_last, preferred_element_type=jnp.float32)
    return placed, ids, within


def place_kernel(groups, spot_ref, emb_ref, name_ref, main_ref, tail_ref, ids_ref, within_ref):
    placed, ids, within = put_rows(groups, 0, spot_ref, emb_ref, name_ref)
    width = main_ref.shape[1]
    for start in range(0, width, wide):
        size = min(wide, width - start)
        main_ref[:, start : start + size] = placed(start, size)
    tail_ref[...] = placed(width, tail)
    ids_ref[...] = ids
    within_ref[...] = within


def pair_kernel(
    groups, spot_ref, emb_ref, name_ref, first_ref, last_ref, ids_ref, main_ref, tail_ref
):
    placed, ids, _ = put_rows(groups, 1, spot_ref, emb_ref, name_ref)
    teams, _, width = main_ref.shape
    main_ref[:, :capacity, :] = first_ref[...].reshape(teams, capacity, width)
    tail_ref[:, :capacity, :] = last_ref[...].reshape(teams, capacity, tail)
    for start in range(0, width, wide):
        size = min(wide, width - start)
        main_ref[:, capacity:field, start : start + size] = placed(start, size).reshape(
            teams, capacity, size
        )
    tail_ref[:, capacity:field, :] = placed(width, tail).reshape(teams, capacity, tail)
    ids = (ids + ids_ref[...] - 1.0).astype(jnp.bfloat16)
    tail_ref[:, field:, :] = jnp.broadcast_to(ids[:, None, :], (teams, note, lanes))


def read_ids(ref, hold):
    count = lanes // field
    blocks = ref.shape[0] // count
    hold[...] = jnp.max(ref[:, field:, :].astype(jnp.float32), axis=1)
    lane = lax.broadcasted_iota(jnp.int32, (blocks, lanes), 1)
    total = hold[pl.ds(0, blocks, stride=count), :]
    for q in range(1, count):
        piece = pltpu.roll(hold[pl.ds(q, blocks, stride=count), :], field * q, 1)
        total = jnp.where(lane // field == q, piece, total)
    return total


def features(main, last, start, count):
    rest = last[start // field : (start + count) // field, :field, :].reshape(count, tail)
    return jnp.concatenate([main[start : start + count, :], rest], axis=1)


def to_column(row):
    return jnp.transpose(jnp.broadcast_to(row, (lanes, lanes)))


def columns_of(ids):
    return jnp.concatenate([to_column(ids[b : b + 1, :]) for b in range(ids.shape[0])], axis=0)


def to_rows(tile):
    return jnp.concatenate(
        [
            jnp.max(jnp.transpose(tile[b * lanes : (b + 1) * lanes, :]), axis=0, keepdims=True)
            for b in range(tile.shape[0] // lanes)
        ],
        axis=0,
    )


def product(left, right):
    return lax.dot_general(left, right, contract_last, preferred_element_type=jnp.float32)


def scan_block(total, left_ids, right_ids, best, skip):
    tops = []
    for half in range(wide // lanes):
        scores = total[:, half * lanes : (half + 1) * lanes]
        ids = right_ids[half : half + 1, :]
        same = left_ids == jnp.where(ids < 0, -2.0, ids)
        if skip is not None:
            row = lax.broadcasted_iota(jnp.int32, scores.shape, 0)
            column = lax.broadcasted_iota(jnp.int32, scores.shape, 1)
            same = same & (row - column != skip + half * lanes)
        masked = jnp.where(same, scores, -1.0)
        best = masked if best is None else jnp.maximum(best, masked)
        tops.append(jnp.max(masked, axis=0, keepdims=True))
    return best, tops


def own_kernel(main, last, out_ref, ids_ref, hold):
    ids = read_ids(last, hold)
    ids_ref[...] = ids
    rows = main.shape[0]
    columns = columns_of(ids)
    left = features(main, last, 0, rows)
    best = None
    per = wide // lanes
    for at in range(rows // wide):
        best, _ = scan_block(
            product(left, features(main, last, at * wide, wide)),
            columns,
            ids[at * per : (at + 1) * per, :],
            best,
            at * wide,
        )
    out_ref[...] = to_rows(best)


def start_kernel(spot_ref, main, after, before, near_ref, side_ref):
    low = spot_ref[1] == 1
    rows = main.shape[0]
    left = main[...]
    side_left = jnp.where(low, before[: rows // 2, :], after[rows // 2 :, :])
    for at in range(0, rows, wide):
        near = after[at : at + wide, :]
        near_ref[:, at : at + wide] = product(left, near)
        right = jnp.where(low, near, before[at : at + wide, :])
        side_ref[:, at : at + wide] = product(side_left, right)


def cross_kernel(
    spot_ref,
    last,
    after_last,
    before_last,
    near_ref,
    side_ref,
    inside_ref,
    ids_ref,
    out_ref,
    hold,
    table,
):
    low = spot_ref[1] == 1
    ids, after_ids, before_ids = (
        ids_ref[...],
        read_ids(after_last, hold.at[0]),
        read_ids(before_last, hold.at[1]),
    )
    blocks = ids.shape[0]
    rows = blocks * lanes
    half = rows // 2
    columns = columns_of(ids)
    right_ids = jnp.where(low, after_ids, before_ids)
    left_ids = jnp.where(low, before_ids[: blocks // 2, :], after_ids[blocks // 2 :, :])
    left_columns = columns_of(left_ids)

    def final(ref):
        return ref[:, :field, :].reshape(rows, tail)

    left, after, before = final(last), final(after_last), final(before_last)
    side_left = jnp.where(low, before[:half, :], after[half:, :])
    per = wide // lanes
    best, far, up, side = None, None, [], []
    for at in range(rows // wide):
        span = slice(at * wide, (at + 1) * wide)
        near = after[span, :]
        right = jnp.where(low, near, before[span, :])
        cut = slice(at * per, (at + 1) * per)
        best, tops = scan_block(
            near_ref[:, span] + product(left, near), columns, after_ids[cut, :], best, None)
        up += tops
        far, tops = scan_block(
            side_ref[:, span] + product(side_left, right), left_columns, right_ids[cut, :], far, None)
        side += tops
    up, side = jnp.concatenate(up, axis=0), jnp.concatenate(side, axis=0)
    mine = jnp.maximum(to_rows(best), inside_ref[...])
    found = to_rows(far)
    blank = jnp.full(found.shape, -1.0, jnp.float32)
    placed = jnp.where(
        low, jnp.concatenate([found, blank], axis=0), jnp.concatenate([blank, found], axis=0)
    )
    up = jnp.maximum(up, jnp.where(low, side, placed))
    down = jnp.where(low, placed, side)
    count = lanes // field
    steps = (0, 1, places - 1)
    for step, values in enumerate((mine, up, down)):
        for q in range(count):
            turned = values if q == 0 else pltpu.roll(values, lanes - field * q, 1)
            table[step, pl.ds(q, blocks, stride=count), :] = turned
    core, x, y = spot_ref[0], spot_ref[2], spot_ref[3]
    each = places * depth
    across = cores * places

    def found(step, other):
        values = table[step]
        return jnp.where(other == core, values, pltpu.roll(values, lanes - capacity, 1))

    @pl.when(core == 0)
    def _():
        for step, move in enumerate(steps):
            for other in range(cores):
                start = other * places + lax.rem(x + move, places)
                out_ref[pl.ds(start, each, stride=across), :] = found(step, other)

    @pl.when(core == 1)
    def _():
        for step, move in enumerate(steps):
            row = lax.rem(y + move, places) * (depth * across)
            for other in range(cores):
                values = found(step, other)
                for place in range(places):
                    start = row + other * places + place
                    out_ref[pl.ds(start, depth, stride=across), :] = values[
                        place * depth : (place + 1) * depth, :
                    ]


def fetch_kernel(spot_ref, back_ref, name_ref, within_ref, out_ref):
    x, y = spot_ref[2], spot_ref[3]
    each = places * depth
    across = cores * places
    even, odd = None, []
    for move in (0, 1, places - 1):
        rows = back_ref[pl.ds(lax.rem(x + move, places), each, stride=across), :]
        even = rows if even is None else jnp.maximum(even, rows)
    for place in range(places):
        total = None
        for move in (0, 1, places - 1):
            start = lax.rem(y + move, places) * (depth * across) + places + place
            rows = back_ref[pl.ds(start, depth, stride=across), :]
            total = rows if total is None else jnp.maximum(total, rows)
        odd.append(total)
    odd = pltpu.roll(jnp.concatenate(odd, axis=0), capacity, 1)
    rest = jnp.where(lax.broadcasted_iota(jnp.int32, even.shape, 1) < capacity, even, odd)
    rest = jnp.where(lax.broadcasted_iota(jnp.int32, even.shape, 1) < field, rest, 0.0)
    owner = name_ref[...] // labels
    rows = owner.shape[1]
    team = lax.broadcasted_iota(jnp.int32, (places * depth, rows), 0)
    onehot = (team == owner // cores).astype(jnp.bfloat16)
    found = jnp.zeros((lanes, rows), jnp.float32)
    for _ in range(3):
        piece = rest.astype(jnp.bfloat16)
        rest = rest - piece.astype(jnp.float32)
        found = found + lax.dot_general(
            piece, onehot, (((0,), (0,)), ((), ())), preferred_element_type=jnp.float32
        )
    lane = lax.broadcasted_iota(jnp.int32, (lanes, rows), 0)
    within = within_ref[...] + owner % cores * capacity
    out_ref[...] = jnp.sum(jnp.where(lane == within, found, 0.0), axis=0, keepdims=True)


def send(values, route):
    return lax.ppermute(values, everyone, route)


def trade(values, teams):
    return lax.all_to_all(
        values, everyone, split_axis=0, concat_axis=0, axis_index_groups=teams, tiled=True
    )


def shards(embeddings, owner, cluster):
    rows, width = embeddings.shape
    groups = lax.axis_size("ingest")
    spots = groups * capacity
    blocks = spots // lanes
    each = places * depth
    f32 = jnp.float32
    at, x = lax.axis_index("ingest"), lax.axis_index("span")
    core, y = at % cores, at // (cores * depth)
    low = jnp.where(core == 0, x, y) < places // 2
    spot = jnp.stack([core, low.astype(jnp.int32), x, y]).astype(jnp.int32)
    smem, vmem = pl.BlockSpec(memory_space=pltpu.SMEM), pl.BlockSpec(memory_space=pltpu.VMEM)

    def call(kernel, out_shape, name, *args, scratch=()):
        return pl.pallas_call(
            kernel,
            out_shape=out_shape,
            in_specs=[smem if a is spot else vmem for a in args],
            scratch_shapes=scratch,
            compiler_params=params(),
            name=name,
        )(*args)

    def array(*shape, dtype=jnp.bfloat16):
        return jax.ShapeDtypeStruct(shape, dtype)

    swap = other_core()
    cluster = lax.optimization_barrier(cluster.reshape(rows, 1))
    names = (owner * labels + cluster).reshape(1, rows)
    other_rows = send(embeddings, swap)
    other_names = send(names, swap)
    first, last, ids, within = call(
        functools.partial(place_kernel, groups),
        [
            array(spots // cores, width - tail),
            array(spots // cores, tail),
            array(each, lanes, dtype=f32),
            array(1, rows, dtype=jnp.int32),
        ],
        "place",
        spot,
        embeddings,
        names,
    )
    parts = call(
        functools.partial(pair_kernel, groups),
        [array(each, field, width - tail), array(each, field + note, tail)],
        "pair",
        spot,
        other_rows,
        other_names,
        first,
        last,
        ids,
    )
    teams = plane_teams()
    own, after, before = [], [], []
    for part in parts:
        got = trade(part, teams)
        if not own:
            got = got.reshape(spots, width - tail)
        own.append(got)
        before.append(send(got, beside(1)))
        after.append(send(got, beside(-1)))
    inside, ids = call(
        own_kernel,
        [array(blocks, lanes, dtype=f32)] * 2,
        "own",
        *own,
        scratch=[pltpu.VMEM((each, lanes), f32)],
    )
    count = groups * places
    near, side = call(
        start_kernel,
        [array(spots, spots, dtype=f32), array(spots // 2, spots, dtype=f32)],
        "start",
        spot,
        own[0],
        after[0],
        before[0],
    )
    best = call(
        cross_kernel,
        array(count, lanes, dtype=f32),
        "cross",
        spot,
        own[1],
        after[1],
        before[1],
        near,
        side,
        inside,
        ids,
        scratch=[pltpu.VMEM((2, each, lanes), f32), pltpu.VMEM((3, each, lanes), f32)],
    )
    back = lax.all_to_all(
        best.reshape(count, 1, 1, lanes), everyone, split_axis=0, concat_axis=0, tiled=True
    ).reshape(count, lanes)
    result = call(fetch_kernel, array(1, rows, dtype=f32), "fetch", spot, back, names, within)
    return result.reshape(rows)


def solution(mesh):
    placed = (P(("ingest", "span"), None), P(("ingest", "span"), None), P(("ingest", "span")))
    return jax.shard_map(
        shards, mesh=mesh, in_specs=placed, out_specs=P(("ingest", "span")), check_vma=False
    )
```

```python
import functools

import jax
import jax.numpy as jnp
from jax import lax
from jax.experimental import pallas as pl
from jax.experimental.pallas import tpu as pltpu
from jax.sharding import PartitionSpec as P

epsilon = 1e-06
capacity = 16
lanes = 128
wide = 256
cores = 2
places = 4
depth = 8
field = cores * capacity
first_rows = 208
note = 8
early = 6
labels = 64
contract_last = (((1,), (1,)), ((), ()))
contract_first = (((1,), (0,)), ((), ()))
everyone = ("ingest", "span")


def params():
    return pltpu.CompilerParams(vmem_limit_bytes=40 * 1024 * 1024)


def device(y, z, core, x):
    return ((y * depth + z) * cores + core) * places + x


def pairs(move):
    found = []
    for y in range(places):
        for z in range(depth):
            for core in range(cores):
                for x in range(places):
                    found.append((device(y, z, core, x), device(*move(y, z, core, x))))
    return found


def other_core():
    return pairs(lambda y, z, core, x: (y, z, 1 - core, x))


def beside(step):
    return pairs(
        lambda y, z, core, x: (y, z, core, (x + step) % places)
        if core == 0
        else ((y + step) % places, z, core, x)
    )


def plane_teams():
    spots, levels = range(places), range(depth)
    return [[device(i, z, 0, x) for i in spots for z in levels] for x in spots] + [
        [device(y, z, 1, i) for i in spots for z in levels] for y in spots
    ]


def rank_rows(owner, groups):
    rows = owner.shape[1]
    belongs = lax.broadcasted_iota(jnp.int32, (groups, rows), 0) == owner
    onehot = belongs.astype(jnp.bfloat16)
    earlier = lax.broadcasted_iota(jnp.int32, (rows, rows), 0) < lax.broadcasted_iota(
        jnp.int32, (rows, rows), 1
    )
    before = lax.dot_general(
        onehot, earlier.astype(jnp.bfloat16), contract_first, preferred_element_type=jnp.float32
    )
    return jnp.sum(jnp.where(belongs, before, 0.0), axis=0, keepdims=True).astype(jnp.int32)


def put_rows(groups, side, spot_ref, emb_ref, name_ref):
    core = spot_ref[0]
    owner = name_ref[...] // labels
    rows = owner.shape[1]
    within = rank_rows(owner, groups)
    slot = jnp.where(owner % cores == core, owner // cores * capacity + within, -1)
    room = groups // cores * capacity
    put = (lax.broadcasted_iota(jnp.int32, (room, rows), 0) == slot).astype(jnp.bfloat16)
    values = emb_ref[...].astype(jnp.float32)
    squared = jnp.sum(values * values, axis=1, keepdims=True)
    unit = (values * lax.rsqrt(squared + epsilon)).astype(jnp.bfloat16)

    def placed(start, width):
        return lax.dot_general(
            put,
            unit[:, start : start + width],
            contract_first,
            preferred_element_type=jnp.float32,
        ).astype(jnp.bfloat16)

    team = lax.broadcasted_iota(jnp.int32, (groups // cores, rows), 0)
    here = (team == owner // cores) & (owner % cores == core)
    named = here.astype(jnp.bfloat16) * (name_ref[...] % labels + 1).astype(jnp.bfloat16)
    lane = lax.broadcasted_iota(jnp.int32, (lanes, rows), 0)
    into = (lane == within + side * capacity).astype(jnp.bfloat16)
    ids = lax.dot_general(named, into, contract_last, preferred_element_type=jnp.float32)
    return placed, ids, within


def place_kernel(groups, spot_ref, emb_ref, name_ref, half_ref, ids_ref, within_ref):
    placed, ids, within = put_rows(groups, 0, spot_ref, emb_ref, name_ref)
    teams, count, _ = half_ref.shape
    for start in range(0, count // capacity * lanes, wide):
        values = placed(start, wide)
        for shift in range(0, wide, lanes):
            at = (start + shift) // lanes * capacity
            half_ref[:, at : at + capacity, :] = values[:, shift : shift + lanes].reshape(
                teams, capacity, lanes
            )
    ids_ref[...] = ids
    within_ref[...] = within


def pair_kernel(groups, spot_ref, emb_ref, name_ref, half_ref, ids_ref, main_ref, last_ref):
    placed, ids, _ = put_rows(groups, 1, spot_ref, emb_ref, name_ref)
    teams, count, _ = half_ref.shape
    border = main_ref.shape[1]

    def store(at, values):
        if at < border:
            main_ref[:, at : at + capacity, :] = values
        else:
            last_ref[:, at - border : at - border + capacity, :] = values

    for start in range(0, count // capacity * lanes, wide):
        values = placed(start, wide)
        for shift in range(0, wide, lanes):
            block = (start + shift) // lanes
            store(block * field, half_ref[:, block * capacity : (block + 1) * capacity, :])
            store(
                block * field + capacity,
                values[:, shift : shift + lanes].reshape(teams, capacity, lanes),
            )
    ids = (ids + ids_ref[...] - 1.0).astype(jnp.bfloat16)
    last_ref[:, last_ref.shape[1] - note :, :] = jnp.broadcast_to(
        ids[:, None, :], (teams, note, lanes)
    )


def read_ids(ref, hold):
    count = lanes // field
    blocks = ref.shape[0] // count
    hold[...] = jnp.max(ref[:, ref.shape[1] - note :, :].astype(jnp.float32), axis=1)
    lane = lax.broadcasted_iota(jnp.int32, (blocks, lanes), 1)
    total = hold[pl.ds(0, blocks, stride=count), :]
    for q in range(1, count):
        piece = pltpu.roll(hold[pl.ds(q, blocks, stride=count), :], field * q, 1)
        total = jnp.where(lane // field == q, piece, total)
    return total


def features(main, last, blocks, start, count):
    teams = slice(start // field, (start + count) // field)
    border = main.shape[1]
    found = []
    for block in blocks:
        low, high = block * field, (block + 1) * field
        parts = []
        if low < border:
            parts.append(main[teams, low : min(high, border), :])
        if high > border:
            parts.append(last[teams, max(low, border) - border : high - border, :])
        piece = parts[0] if len(parts) == 1 else jnp.concatenate(parts, axis=1)
        found.append(piece.reshape(count, lanes))
    return jnp.concatenate(found, axis=1)


def to_column(row):
    return jnp.transpose(jnp.broadcast_to(row, (lanes, lanes)))


def columns_of(ids):
    return jnp.concatenate([to_column(ids[b : b + 1, :]) for b in range(ids.shape[0])], axis=0)


def to_rows(tile):
    return jnp.concatenate(
        [
            jnp.max(jnp.transpose(tile[b * lanes : (b + 1) * lanes, :]), axis=0, keepdims=True)
            for b in range(tile.shape[0] // lanes)
        ],
        axis=0,
    )


def product(left, right):
    return lax.dot_general(left, right, contract_last, preferred_element_type=jnp.float32)


def scan_block(total, left_ids, right_ids, best, skip):
    tops = []
    for half in range(wide // lanes):
        scores = total[:, half * lanes : (half + 1) * lanes]
        ids = right_ids[half : half + 1, :]
        same = left_ids == jnp.where(ids < 0, -2.0, ids)
        if skip is not None:
            row = lax.broadcasted_iota(jnp.int32, scores.shape, 0)
            column = lax.broadcasted_iota(jnp.int32, scores.shape, 1)
            same = same & (row - column != skip + half * lanes)
        masked = jnp.where(same, scores, -1.0)
        best = masked if best is None else jnp.maximum(best, masked)
        tops.append(jnp.max(masked, axis=0, keepdims=True))
    return best, tops


def own_kernel(main, last, out_ref, ids_ref, hold):
    ids = read_ids(last, hold)
    ids_ref[...] = ids
    rows = ids.shape[0] * lanes
    blocks = range((main.shape[1] + last.shape[1] - note) // field)
    columns = columns_of(ids)
    left = features(main, last, blocks, 0, rows)
    best = None
    per = wide // lanes
    for at in range(rows // wide):
        best, _ = scan_block(
            product(left, features(main, last, blocks, at * wide, wide)),
            columns,
            ids[at * per : (at + 1) * per, :],
            best,
            at * wide,
        )
    out_ref[...] = to_rows(best)


def start_kernel(spot_ref, main, after, before, near_ref, side_ref):
    low = spot_ref[1] == 1
    rows = main.shape[0] * field
    half = rows // 2
    blocks = range(early)
    left = features(main, None, blocks, 0, rows)
    side_left = jnp.where(
        low, features(before, None, blocks, 0, half), features(after, None, blocks, half, half)
    )
    for at in range(0, rows, wide):
        near = features(after, None, blocks, at, wide)
        near_ref[:, at : at + wide] = product(left, near)
        right = jnp.where(low, near, features(before, None, blocks, at, wide))
        side_ref[:, at : at + wide] = product(side_left, right)


def cross_kernel(
    spot_ref,
    main,
    last,
    after_main,
    after_last,
    before_main,
    before_last,
    near_ref,
    side_ref,
    inside_ref,
    ids_ref,
    out_ref,
    hold,
    table,
):
    low = spot_ref[1] == 1
    ids, after_ids, before_ids = (
        ids_ref[...],
        read_ids(after_last, hold.at[0]),
        read_ids(before_last, hold.at[1]),
    )
    blocks = ids.shape[0]
    rows = blocks * lanes
    half = rows // 2
    late = range(early, (main.shape[1] + last.shape[1] - note) // field)
    left = features(main, last, late, 0, rows)
    after = features(after_main, after_last, late, 0, rows)
    before = features(before_main, before_last, late, 0, rows)
    side_left = jnp.where(low, before[:half, :], after[half:, :])
    columns = columns_of(ids)
    right_ids = jnp.where(low, after_ids, before_ids)
    left_ids = jnp.where(low, before_ids[: blocks // 2, :], after_ids[blocks // 2 :, :])
    left_columns = columns_of(left_ids)
    per = wide // lanes
    best, far, up, side = None, None, [], []
    for at in range(rows // wide):
        span = slice(at * wide, (at + 1) * wide)
        near = after[span, :]
        right = jnp.where(low, near, before[span, :])
        cut = slice(at * per, (at + 1) * per)
        best, tops = scan_block(
            near_ref[:, span] + product(left, near), columns, after_ids[cut, :], best, None)
        up += tops
        far, tops = scan_block(
            side_ref[:, span] + product(side_left, right), left_columns, right_ids[cut, :], far, None)
        side += tops
    up, side = jnp.concatenate(up, axis=0), jnp.concatenate(side, axis=0)
    mine = jnp.maximum(to_rows(best), inside_ref[...])
    found = to_rows(far)
    blank = jnp.full(found.shape, -1.0, jnp.float32)
    placed = jnp.where(
        low, jnp.concatenate([found, blank], axis=0), jnp.concatenate([blank, found], axis=0)
    )
    up = jnp.maximum(up, jnp.where(low, side, placed))
    down = jnp.where(low, placed, side)
    count = lanes // field
    steps = (0, 1, places - 1)
    for step, values in enumerate((mine, up, down)):
        for q in range(count):
            turned = values if q == 0 else pltpu.roll(values, lanes - field * q, 1)
            table[step, pl.ds(q, blocks, stride=count), :] = turned
    core, x, y = spot_ref[0], spot_ref[2], spot_ref[3]
    each = places * depth
    across = cores * places

    def found(step, other):
        values = table[step]
        return jnp.where(other == core, values, pltpu.roll(values, lanes - capacity, 1))

    @pl.when(core == 0)
    def _():
        for step, move in enumerate(steps):
            for other in range(cores):
                start = other * places + lax.rem(x + move, places)
                out_ref[pl.ds(start, each, stride=across), :] = found(step, other)

    @pl.when(core == 1)
    def _():
        for step, move in enumerate(steps):
            row = lax.rem(y + move, places) * (depth * across)
            for other in range(cores):
                values = found(step, other)
                for place in range(places):
                    start = row + other * places + place
                    out_ref[pl.ds(start, depth, stride=across), :] = values[
                        place * depth : (place + 1) * depth, :
                    ]


def fetch_kernel(spot_ref, back_ref, name_ref, within_ref, out_ref):
    x, y = spot_ref[2], spot_ref[3]
    each = places * depth
    across = cores * places
    even, odd = None, []
    for move in (0, 1, places - 1):
        rows = back_ref[pl.ds(lax.rem(x + move, places), each, stride=across), :]
        even = rows if even is None else jnp.maximum(even, rows)
    for place in range(places):
        total = None
        for move in (0, 1, places - 1):
            start = lax.rem(y + move, places) * (depth * across) + places + place
            rows = back_ref[pl.ds(start, depth, stride=across), :]
            total = rows if total is None else jnp.maximum(total, rows)
        odd.append(total)
    odd = pltpu.roll(jnp.concatenate(odd, axis=0), capacity, 1)
    rest = jnp.where(lax.broadcasted_iota(jnp.int32, even.shape, 1) < capacity, even, odd)
    rest = jnp.where(lax.broadcasted_iota(jnp.int32, even.shape, 1) < field, rest, 0.0)
    owner = name_ref[...] // labels
    rows = owner.shape[1]
    team = lax.broadcasted_iota(jnp.int32, (places * depth, rows), 0)
    onehot = (team == owner // cores).astype(jnp.bfloat16)
    pieces = []
    for _ in range(3):
        pieces.append(rest.astype(jnp.bfloat16))
        rest = rest - pieces[-1].astype(jnp.float32)
    found = lax.dot_general(
        jnp.concatenate(pieces, axis=0),
        jnp.concatenate([onehot] * 3, axis=0),
        (((0,), (0,)), ((), ())),
        preferred_element_type=jnp.float32,
    )[:field, :]
    lane = lax.broadcasted_iota(jnp.int32, (field, rows), 0)
    within = within_ref[...] + owner % cores * capacity
    out_ref[...] = jnp.sum(jnp.where(lane == within, found, 0.0), axis=0, keepdims=True)


def send(values, route):
    return lax.ppermute(values, everyone, route)


def trade(values, teams):
    return lax.all_to_all(
        values, everyone, split_axis=0, concat_axis=0, axis_index_groups=teams, tiled=True
    )


def shards(embeddings, owner, cluster):
    rows, width = embeddings.shape
    groups = lax.axis_size("ingest")
    spots = groups * capacity
    blocks = spots // lanes
    each = places * depth
    f32 = jnp.float32
    at, x = lax.axis_index("ingest"), lax.axis_index("span")
    core, y = at % cores, at // (cores * depth)
    low = jnp.where(core == 0, x, y) < places // 2
    spot = jnp.stack([core, low.astype(jnp.int32), x, y]).astype(jnp.int32)
    smem, vmem = pl.BlockSpec(memory_space=pltpu.SMEM), pl.BlockSpec(memory_space=pltpu.VMEM)

    def call(kernel, out_shape, name, *args, scratch=()):
        return pl.pallas_call(
            kernel,
            out_shape=out_shape,
            in_specs=[smem if a is spot else vmem for a in args],
            scratch_shapes=scratch,
            compiler_params=params(),
            name=name,
        )(*args)

    def array(*shape, dtype=jnp.bfloat16):
        return jax.ShapeDtypeStruct(shape, dtype)

    swap = other_core()
    cluster = lax.optimization_barrier(cluster.reshape(rows, 1))
    names = (owner * labels + cluster).reshape(1, rows)
    other_rows = send(embeddings, swap)
    other_names = send(names, swap)
    total = width // lanes * field
    half, ids, within = call(
        functools.partial(place_kernel, groups),
        [
            array(each, total // cores, lanes),
            array(each, lanes, dtype=f32),
            array(1, rows, dtype=jnp.int32),
        ],
        "place",
        spot,
        embeddings,
        names,
    )
    parts = call(
        functools.partial(pair_kernel, groups),
        [array(each, first_rows, lanes), array(each, total - first_rows + note, lanes)],
        "pair",
        spot,
        other_rows,
        other_names,
        half,
        ids,
    )
    teams = plane_teams()
    own, after, before = [], [], []
    for part in parts:
        got = trade(part, teams)
        own.append(got)
        before.append(send(got, beside(1)))
        after.append(send(got, beside(-1)))
    inside, ids = call(
        own_kernel,
        [array(blocks, lanes, dtype=f32)] * 2,
        "own",
        *own,
        scratch=[pltpu.VMEM((each, lanes), f32)],
    )
    count = groups * places
    near, side = call(
        start_kernel,
        [array(spots, spots, dtype=f32), array(spots // 2, spots, dtype=f32)],
        "start",
        spot,
        own[0],
        after[0],
        before[0],
    )
    best = call(
        cross_kernel,
        array(count, lanes, dtype=f32),
        "cross",
        spot,
        *own,
        *after,
        *before,
        near,
        side,
        inside,
        ids,
        scratch=[pltpu.VMEM((2, each, lanes), f32), pltpu.VMEM((3, each, lanes), f32)],
    )
    back = lax.all_to_all(
        best.reshape(count, 1, 1, lanes), everyone, split_axis=0, concat_axis=0, tiled=True
    ).reshape(count, lanes)
    result = call(fetch_kernel, array(1, rows, dtype=f32), "fetch", spot, back, names, within)
    return result.reshape(rows)


def solution(mesh):
    placed = (P(("ingest", "span"), None), P(("ingest", "span"), None), P(("ingest", "span")))
    return jax.shard_map(
        shards, mesh=mesh, in_specs=placed, out_specs=P(("ingest", "span")), check_vma=False
    )
```

```python
import functools

import jax
import jax.numpy as jnp
from jax import lax
from jax.experimental import pallas as pl
from jax.experimental.pallas import tpu as pltpu
from jax.sharding import PartitionSpec as P

epsilon = 1e-06
capacity = 16
lanes = 128
wide = 256
cores = 2
places = 4
depth = 8
field = cores * capacity
note = 8
early = 6
first_rows = 208
nowhere = -4.0
labels = 64
label_bits, core_bits, field_bits = 6, 1, 5
contract_last = (((1,), (1,)), ((), ()))
contract_first = (((1,), (0,)), ((), ()))
everyone = ("ingest", "span")


def params():
    return pltpu.CompilerParams(vmem_limit_bytes=40 * 1024 * 1024)


def device(y, z, core, x):
    return ((y * depth + z) * cores + core) * places + x


def pairs(move):
    found = []
    for y in range(places):
        for z in range(depth):
            for core in range(cores):
                for x in range(places):
                    found.append((device(y, z, core, x), device(*move(y, z, core, x))))
    return found


def other_core():
    return pairs(lambda y, z, core, x: (y, z, 1 - core, x))


def beside(step):
    return pairs(
        lambda y, z, core, x: (y, z, core, (x + step) % places)
        if core == 0
        else ((y + step) % places, z, core, x)
    )


def plane_teams():
    spots, levels = range(places), range(depth)
    return [[device(i, z, 0, x) for i in spots for z in levels] for x in spots] + [
        [device(y, z, 1, i) for i in spots for z in levels] for y in spots
    ]


def rank_rows(owner, groups):
    rows = owner.shape[1]
    belongs = lax.broadcasted_iota(jnp.int32, (groups, rows), 0) == owner
    onehot = belongs.astype(jnp.bfloat16)
    earlier = lax.broadcasted_iota(jnp.int32, (rows, rows), 0) < lax.broadcasted_iota(
        jnp.int32, (rows, rows), 1
    )
    before = lax.dot_general(
        onehot, earlier.astype(jnp.bfloat16), contract_first, preferred_element_type=jnp.float32
    )
    return jnp.sum(jnp.where(belongs, before, 0.0), axis=0, keepdims=True).astype(jnp.int32)


def put_rows(groups, side, spot_ref, emb_ref, name_ref):
    core = spot_ref[0]
    owner = name_ref[...] >> label_bits
    rows = owner.shape[1]
    within = rank_rows(owner, groups)
    slot = jnp.where((owner & (cores - 1)) == core, (owner >> core_bits) * capacity + within, -1)
    room = groups // cores * capacity
    put = (lax.broadcasted_iota(jnp.int32, (room, rows), 0) == slot).astype(jnp.bfloat16)
    values = emb_ref[...].astype(jnp.float32)
    squared = jnp.sum(values * values, axis=1, keepdims=True)
    unit = (values * lax.rsqrt(squared + epsilon)).astype(jnp.bfloat16)

    def placed(start, width):
        return lax.dot_general(
            put,
            unit[:, start : start + width],
            contract_first,
            preferred_element_type=jnp.float32,
        ).astype(jnp.bfloat16)

    team = lax.broadcasted_iota(jnp.int32, (groups // cores, rows), 0)
    here = (team == (owner >> core_bits)) & ((owner & (cores - 1)) == core)
    named = here.astype(jnp.bfloat16) * ((name_ref[...] & (labels - 1)) + 1).astype(jnp.bfloat16)
    lane = lax.broadcasted_iota(jnp.int32, (lanes, rows), 0)
    into = (lane == within + side * capacity).astype(jnp.bfloat16)
    ids = lax.dot_general(named, into, contract_last, preferred_element_type=jnp.float32)
    return placed, ids, within


def place_kernel(groups, spot_ref, emb_ref, name_ref, half_ref, ids_ref, within_ref):
    placed, ids, within = put_rows(groups, 0, spot_ref, emb_ref, name_ref)
    teams, count, _ = half_ref.shape
    for start in range(0, count // capacity * lanes, wide):
        values = placed(start, wide)
        for shift in range(0, wide, lanes):
            at = (start + shift) // lanes * capacity
            half_ref[:, at : at + capacity, :] = values[:, shift : shift + lanes].reshape(
                teams, capacity, lanes
            )
    ids_ref[...] = ids
    within_ref[...] = within


def pair_kernel(groups, spot_ref, emb_ref, name_ref, half_ref, ids_ref, main_ref, last_ref):
    placed, ids, _ = put_rows(groups, 1, spot_ref, emb_ref, name_ref)
    teams, count, _ = half_ref.shape
    border = main_ref.shape[1] - note

    def store(at, values):
        if at < border:
            main_ref[:, at : at + capacity, :] = values
        else:
            last_ref[:, at - border : at - border + capacity, :] = values

    for start in range(0, count // capacity * lanes, wide):
        values = placed(start, wide)
        for shift in range(0, wide, lanes):
            block = (start + shift) // lanes
            store(block * field, half_ref[:, block * capacity : (block + 1) * capacity, :])
            store(
                block * field + capacity,
                values[:, shift : shift + lanes].reshape(teams, capacity, lanes),
            )
    ids = (ids + ids_ref[...] - 1.0).astype(jnp.bfloat16)
    main_ref[:, border:, :] = jnp.broadcast_to(
        ids[:, None, :], (teams, note, lanes)
    )


def read_ids(ref, hold):
    count = lanes // field
    blocks = ref.shape[0] // count
    hold[...] = jnp.max(ref[:, ref.shape[1] - note :, :].astype(jnp.float32), axis=1)
    lane = lax.broadcasted_iota(jnp.int32, (blocks, lanes), 1)
    total = hold[pl.ds(0, blocks, stride=count), :]
    for q in range(1, count):
        piece = pltpu.roll(hold[pl.ds(q, blocks, stride=count), :], field * q, 1)
        total = jnp.where(lane >> field_bits == q, piece, total)
    return total


def features(refs, blocks, start, count):
    teams = slice(start // field, (start + count) // field)
    found = []
    for block in blocks:
        low, high = block * field, (block + 1) * field
        parts = []
        if low < first_rows:
            parts.append(refs[0][teams, low : min(high, first_rows), :])
        if high > first_rows:
            parts.append(refs[1][teams, max(low, first_rows) - first_rows : high - first_rows, :])
        piece = parts[0] if len(parts) == 1 else jnp.concatenate(parts, axis=1)
        found.append(piece.reshape(count, lanes))
    return jnp.concatenate(found, axis=1)


def to_column(row):
    return jnp.transpose(jnp.broadcast_to(row, (lanes, lanes)))


def columns_of(ids):
    return jnp.concatenate([to_column(ids[b : b + 1, :]) for b in range(ids.shape[0])], axis=0)


def to_rows(tile):
    return jnp.concatenate(
        [
            jnp.max(jnp.transpose(tile[b * lanes : (b + 1) * lanes, :]), axis=0, keepdims=True)
            for b in range(tile.shape[0] // lanes)
        ],
        axis=0,
    )


def product(left, right):
    return lax.dot_general(left, right, contract_last, preferred_element_type=jnp.float32)


def own_kernel(main, last, out_ref, hold):
    ids = read_ids(main, hold)
    rows = ids.shape[0] * lanes
    blocks = range((first_rows + last.shape[1]) // field)
    columns = columns_of(ids)
    left = features((main, last), blocks, 0, rows)
    steps, per = rows // wide, wide // lanes
    best, tops = [None] * steps, []
    for at in range(steps):
        begin = at * wide
        masked = []
        total = product(left[begin:, :], left[begin : begin + wide, :])
        for h in range(per):
            scores = total[:, h * lanes : (h + 1) * lanes]
            row_ids = ids[at * per + h : at * per + h + 1, :]
            row = lax.broadcasted_iota(jnp.int32, scores.shape, 0)
            column = lax.broadcasted_iota(jnp.int32, scores.shape, 1)
            same = columns[begin:, :] == jnp.where(row_ids < 0, -2.0, row_ids)
            masked.append(jnp.where(same & (row - column != h * lanes), scores, -1.0))
            tops.append(jnp.max(masked[-1], axis=0, keepdims=True))
        both = jnp.maximum(masked[0], masked[1])
        for i in range(at, steps):
            part = both[i * wide - begin : (i + 1) * wide - begin, :]
            best[i] = part if best[i] is None else jnp.maximum(best[i], part)
    out_ref[...] = jnp.maximum(
        to_rows(jnp.concatenate(best, axis=0)), jnp.concatenate(tops, axis=0)
    )


def masked_sums(sums, left_ids, right_ids):
    return jnp.concatenate(
        [
            jnp.where(
                left_ids == jnp.where(right_ids[h : h + 1, :] < 0, -2.0, right_ids[h : h + 1, :]),
                sums[:, h * lanes : (h + 1) * lanes],
                nowhere,
            )
            for h in range(wide // lanes)
        ],
        axis=1,
    )


def start_kernel(spot_ref, main, after, before, near_ref, side_ref, hold):
    low = spot_ref[1] == 1
    ids, after_ids, before_ids = [
        read_ids(ref, hold.at[i]) for i, ref in enumerate((main, after, before))
    ]
    count = ids.shape[0]
    rows = count * lanes
    half = rows // 2
    columns = columns_of(ids)
    right_ids = jnp.where(low, after_ids, before_ids)
    left_ids = jnp.where(low, before_ids[: count // 2, :], after_ids[count // 2 :, :])
    left_columns = columns_of(left_ids)
    blocks = range(early)
    left = features((main,), blocks, 0, rows)
    side_left = jnp.where(
        low, features((before,), blocks, 0, half), features((after,), blocks, half, half)
    )
    per = wide // lanes
    for at in range(rows // wide):
        span, cut = slice(at * wide, (at + 1) * wide), slice(at * per, (at + 1) * per)
        near = features((after,), blocks, at * wide, wide)
        near_ref[:, span] = masked_sums(product(left, near), columns, after_ids[cut, :])
        right = jnp.where(low, near, features((before,), blocks, at * wide, wide))
        side_ref[:, span] = masked_sums(
            product(side_left, right), left_columns, right_ids[cut, :]
        )


def add_block(total, best):
    halves = [total[:, h * lanes : (h + 1) * lanes] for h in range(wide // lanes)]
    for part in halves:
        best = part if best is None else jnp.maximum(best, part)
    return best, [jnp.max(part, axis=0, keepdims=True) for part in halves]


def cross_kernel(
    spot_ref,
    main,
    last,
    after_main,
    after_last,
    before_main,
    before_last,
    near_ref,
    side_ref,
    inside_ref,
    out_ref,
    table,
):
    low = spot_ref[1] == 1
    blocks = inside_ref.shape[0]
    rows = blocks * lanes
    half = rows // 2
    late = range(early, (first_rows + last.shape[1]) // field)
    left, after, before = [
        features(refs, late, 0, rows)
        for refs in ((main, last), (after_main, after_last), (before_main, before_last))
    ]
    side_left = jnp.where(low, before[:half, :], after[half:, :])
    best, far, up, side = None, None, [], []
    for at in range(rows // wide):
        span = slice(at * wide, (at + 1) * wide)
        near = after[span, :]
        right = jnp.where(low, near, before[span, :])
        best, tops = add_block(near_ref[:, span] + product(left, near), best)
        up += tops
        far, tops = add_block(side_ref[:, span] + product(side_left, right), far)
        side += tops
    up, side = jnp.concatenate(up, axis=0), jnp.concatenate(side, axis=0)
    mine = jnp.maximum(to_rows(best), inside_ref[...])
    found = to_rows(far)
    blank = jnp.full(found.shape, -1.0, jnp.float32)
    placed = jnp.where(
        low, jnp.concatenate([found, blank], axis=0), jnp.concatenate([blank, found], axis=0)
    )
    up = jnp.maximum(up, jnp.where(low, side, placed))
    down = jnp.where(low, placed, side)
    count = lanes // field
    steps = (0, 1, places - 1)
    for step, values in enumerate((mine, up, down)):
        for q in range(count):
            turned = values if q == 0 else pltpu.roll(values, lanes - field * q, 1)
            table[step, pl.ds(q, blocks, stride=count), :] = turned
    core, x, y = spot_ref[0], spot_ref[2], spot_ref[3]
    each = places * depth
    across = cores * places

    def found(step, other):
        values = table[step]
        return jnp.where(other == core, values, pltpu.roll(values, lanes - capacity, 1))

    @pl.when(core == 0)
    def _():
        for step, move in enumerate(steps):
            for other in range(cores):
                start = other * places + lax.rem(x + move, places)
                out_ref[pl.ds(start, each, stride=across), :] = found(step, other)

    @pl.when(core == 1)
    def _():
        for step, move in enumerate(steps):
            row = lax.rem(y + move, places) * (depth * across)
            for other in range(cores):
                values = found(step, other)
                for place in range(places):
                    start = row + other * places + place
                    out_ref[pl.ds(start, depth, stride=across), :] = values[
                        place * depth : (place + 1) * depth, :
                    ]


def fetch_kernel(spot_ref, back_ref, name_ref, within_ref, out_ref):
    x, y = spot_ref[2], spot_ref[3]
    each = places * depth
    across = cores * places
    even, odd = None, []
    for move in (0, 1, places - 1):
        rows = back_ref[pl.ds(lax.rem(x + move, places), each, stride=across), :]
        even = rows if even is None else jnp.maximum(even, rows)
    for place in range(places):
        total = None
        for move in (0, 1, places - 1):
            start = lax.rem(y + move, places) * (depth * across) + places + place
            rows = back_ref[pl.ds(start, depth, stride=across), :]
            total = rows if total is None else jnp.maximum(total, rows)
        odd.append(total)
    odd = pltpu.roll(jnp.concatenate(odd, axis=0), capacity, 1)
    rest = jnp.where(lax.broadcasted_iota(jnp.int32, even.shape, 1) < capacity, even, odd)
    rest = jnp.where(lax.broadcasted_iota(jnp.int32, even.shape, 1) < field, rest, 0.0)
    owner = name_ref[...] >> label_bits
    rows = owner.shape[1]
    team = lax.broadcasted_iota(jnp.int32, (places * depth, rows), 0)
    onehot = (team == (owner >> core_bits)).astype(jnp.bfloat16)
    pieces = []
    for _ in range(3):
        pieces.append(rest.astype(jnp.bfloat16))
        rest = rest - pieces[-1].astype(jnp.float32)
    found = lax.dot_general(
        jnp.concatenate(pieces, axis=0),
        jnp.concatenate([onehot] * 3, axis=0),
        (((0,), (0,)), ((), ())),
        preferred_element_type=jnp.float32,
    )[:field, :]
    lane = lax.broadcasted_iota(jnp.int32, (field, rows), 0)
    within = within_ref[...] + (owner & (cores - 1)) * capacity
    out_ref[...] = jnp.sum(jnp.where(lane == within, found, 0.0), axis=0, keepdims=True)


def send(values, route):
    return lax.ppermute(values, everyone, route)


def trade(values, teams):
    return lax.all_to_all(
        values, everyone, split_axis=0, concat_axis=0, axis_index_groups=teams, tiled=True
    )


def shards(embeddings, owner, cluster):
    rows, width = embeddings.shape
    groups = lax.axis_size("ingest")
    spots = groups * capacity
    blocks = spots // lanes
    each = places * depth
    f32 = jnp.float32
    at, x = lax.axis_index("ingest"), lax.axis_index("span")
    core, y = at % cores, at // (cores * depth)
    low = jnp.where(core == 0, x, y) < places // 2
    spot = jnp.stack([core, low.astype(jnp.int32), x, y]).astype(jnp.int32)
    smem, vmem = pl.BlockSpec(memory_space=pltpu.SMEM), pl.BlockSpec(memory_space=pltpu.VMEM)

    def call(kernel, out_shape, name, *args, scratch=()):
        return pl.pallas_call(
            kernel,
            out_shape=out_shape,
            in_specs=[smem if a is spot else vmem for a in args],
            scratch_shapes=scratch,
            compiler_params=params(),
            name=name,
        )(*args)

    def array(*shape, dtype=jnp.bfloat16):
        return jax.ShapeDtypeStruct(shape, dtype)

    swap = other_core()
    cluster = lax.optimization_barrier(cluster.reshape(rows, 1))
    names = (owner * labels + cluster).reshape(1, rows)
    other_rows = send(embeddings, swap)
    other_names = send(names, swap)
    total = width // lanes * field
    half, ids, within = call(
        functools.partial(place_kernel, groups),
        [
            array(each, total // cores, lanes),
            array(each, lanes, dtype=f32),
            array(1, rows, dtype=jnp.int32),
        ],
        "place",
        spot,
        embeddings,
        names,
    )
    parts = call(
        functools.partial(pair_kernel, groups),
        [array(each, first_rows + note, lanes), array(each, total - first_rows, lanes)],
        "pair",
        spot,
        other_rows,
        other_names,
        half,
        ids,
    )
    teams = plane_teams()
    own, after, before = [], [], []
    for part in parts:
        got = trade(part, teams)
        own.append(got)
        before.append(send(got, beside(1)))
        after.append(send(got, beside(-1)))
    held = pltpu.VMEM((each, lanes), f32)
    inside = call(own_kernel, array(blocks, lanes, dtype=f32), "own", *own, scratch=[held])
    near, side = call(
        start_kernel,
        [array(spots, spots, dtype=f32), array(spots // 2, spots, dtype=f32)],
        "start",
        spot,
        own[0],
        after[0],
        before[0],
        scratch=[pltpu.VMEM((3, each, lanes), f32)],
    )
    count = groups * places
    best = call(
        cross_kernel,
        array(count, lanes, dtype=f32),
        "cross",
        spot,
        *own,
        *after,
        *before,
        near,
        side,
        inside,
        scratch=[pltpu.VMEM((3, each, lanes), f32)],
    )
    back = lax.all_to_all(
        best.reshape(count, 1, 1, lanes), everyone, split_axis=0, concat_axis=0, tiled=True
    ).reshape(count, lanes)
    result = call(fetch_kernel, array(1, rows, dtype=f32), "fetch", spot, back, names, within)
    return result.reshape(rows)


def solution(mesh):
    placed = (P(("ingest", "span"), None), P(("ingest", "span"), None), P(("ingest", "span")))
    return jax.shard_map(
        shards, mesh=mesh, in_specs=placed, out_specs=P(("ingest", "span")), check_vma=False
    )
```

```python
import functools

import jax
import jax.numpy as jnp
from jax import lax
from jax.experimental import pallas as pl
from jax.experimental.pallas import tpu as pltpu
from jax.sharding import PartitionSpec as P

epsilon = 1e-06
capacity = 16
lanes = 128
wide = 256
cores = 2
places = 4
depth = 8
field = cores * capacity
note = 8
early = 6
first_rows = 208
nowhere = -4.0
core_bits, field_bits = 1, 5
contract_last = (((1,), (1,)), ((), ()))
contract_first = (((1,), (0,)), ((), ()))
everyone = ("ingest", "span")


def params():
    return pltpu.CompilerParams(vmem_limit_bytes=40 * 1024 * 1024)


def device(y, z, core, x):
    return ((y * depth + z) * cores + core) * places + x


def pairs(move):
    found = []
    for y in range(places):
        for z in range(depth):
            for core in range(cores):
                for x in range(places):
                    found.append((device(y, z, core, x), device(*move(y, z, core, x))))
    return found


def other_core():
    return pairs(lambda y, z, core, x: (y, z, 1 - core, x))


def beside(step):
    return pairs(
        lambda y, z, core, x: (y, z, core, (x + step) % places)
        if core == 0
        else ((y + step) % places, z, core, x)
    )


def plane_teams():
    spots, levels = range(places), range(depth)
    return [[device(i, z, 0, x) for i in spots for z in levels] for x in spots] + [
        [device(y, z, 1, i) for i in spots for z in levels] for y in spots
    ]


def rank_rows(owner, groups):
    rows = owner.shape[1]
    belongs = lax.broadcasted_iota(jnp.int32, (groups, rows), 0) == owner
    onehot = belongs.astype(jnp.bfloat16)
    earlier = lax.broadcasted_iota(jnp.int32, (rows, rows), 0) < lax.broadcasted_iota(
        jnp.int32, (rows, rows), 1
    )
    before = lax.dot_general(
        onehot, earlier.astype(jnp.bfloat16), contract_first, preferred_element_type=jnp.float32
    )
    return jnp.sum(jnp.where(belongs, before, 0.0), axis=0, keepdims=True).astype(jnp.int32)


def put_rows(groups, side, spot_ref, emb_ref, owner_ref, cluster_ref):
    core = spot_ref[0]
    owner = owner_ref[...]
    rows = owner.shape[1]
    within = rank_rows(owner, groups)
    slot = jnp.where((owner & (cores - 1)) == core, (owner >> core_bits) * capacity + within, -1)
    room = groups // cores * capacity
    put = (lax.broadcasted_iota(jnp.int32, (room, rows), 0) == slot).astype(jnp.bfloat16)
    values = emb_ref[...].astype(jnp.float32)
    squared = jnp.sum(values * values, axis=1, keepdims=True)
    unit = (values * lax.rsqrt(squared + epsilon)).astype(jnp.bfloat16)

    def placed(start, width):
        return lax.dot_general(
            put,
            unit[:, start : start + width],
            contract_first,
            preferred_element_type=jnp.float32,
        ).astype(jnp.bfloat16)

    team = lax.broadcasted_iota(jnp.int32, (groups // cores, rows), 0)
    here = (team == (owner >> core_bits)) & ((owner & (cores - 1)) == core)
    named = here.astype(jnp.bfloat16) * (cluster_ref[...] + 1).astype(jnp.bfloat16)
    lane = lax.broadcasted_iota(jnp.int32, (lanes, rows), 0)
    into = (lane == within + side * capacity).astype(jnp.bfloat16)
    ids = lax.dot_general(named, into, contract_last, preferred_element_type=jnp.float32)
    return placed, ids, within


def place_kernel(groups, spot_ref, *refs):
    sources, (half_ref, ids_ref, plan_ref), held, done = refs[:3], refs[3:6], refs[6:9], refs[9]
    copies = [
        pltpu.make_async_copy(source, kept, done.at[i])
        for i, (source, kept) in enumerate(zip(sources, held))
    ]
    for copy in copies[::-1]:
        copy.start()
    for copy in copies[::-1]:
        copy.wait()
    placed, ids, within = put_rows(groups, 0, spot_ref, *held)
    teams, count, _ = half_ref.shape
    for start in range(0, count // capacity * lanes, wide):
        values = placed(start, wide)
        for shift in range(0, wide, lanes):
            at = (start + shift) // lanes * capacity
            half_ref[:, at : at + capacity, :] = values[:, shift : shift + lanes].reshape(
                teams, capacity, lanes
            )
    ids_ref[...] = ids
    owner = held[1][...]
    plan_ref[0:1, :] = owner >> core_bits
    plan_ref[1:2, :] = within + (owner & (cores - 1)) * capacity


def pair_kernel(
    groups, spot_ref, emb_ref, owner_ref, cluster_ref, half_ref, ids_ref, main_ref, last_ref
):
    placed, ids, _ = put_rows(groups, 1, spot_ref, emb_ref, owner_ref, cluster_ref)
    teams, count, _ = half_ref.shape
    border = main_ref.shape[1] - note

    def store(at, values):
        if at < border:
            main_ref[:, at : at + capacity, :] = values
        else:
            last_ref[:, at - border : at - border + capacity, :] = values

    for start in range(0, count // capacity * lanes, wide):
        values = placed(start, wide)
        for shift in range(0, wide, lanes):
            block = (start + shift) // lanes
            store(block * field, half_ref[:, block * capacity : (block + 1) * capacity, :])
            store(
                block * field + capacity,
                values[:, shift : shift + lanes].reshape(teams, capacity, lanes),
            )
    ids = (ids + ids_ref[...] - 1.0).astype(jnp.bfloat16)
    main_ref[:, border:, :] = jnp.broadcast_to(
        ids[:, None, :], (teams, note, lanes)
    )


def read_ids(ref, hold):
    count = lanes // field
    blocks = ref.shape[0] // count
    hold[...] = jnp.max(ref[:, ref.shape[1] - note :, :].astype(jnp.float32), axis=1)
    lane = lax.broadcasted_iota(jnp.int32, (blocks, lanes), 1)
    total = hold[pl.ds(0, blocks, stride=count), :]
    for q in range(1, count):
        piece = pltpu.roll(hold[pl.ds(q, blocks, stride=count), :], field * q, 1)
        total = jnp.where(lane >> field_bits == q, piece, total)
    return total


def features(refs, blocks, start, count):
    teams = slice(start // field, (start + count) // field)
    found = []
    for block in blocks:
        low, high = block * field, (block + 1) * field
        parts = []
        if low < first_rows:
            parts.append(refs[0][teams, low : min(high, first_rows), :])
        if high > first_rows:
            parts.append(refs[1][teams, max(low, first_rows) - first_rows : high - first_rows, :])
        piece = parts[0] if len(parts) == 1 else jnp.concatenate(parts, axis=1)
        found.append(piece.reshape(count, lanes))
    return jnp.concatenate(found, axis=1)


def to_column(row):
    return jnp.transpose(jnp.broadcast_to(row, (lanes, lanes)))


def columns_of(ids):
    return jnp.concatenate([to_column(ids[b : b + 1, :]) for b in range(ids.shape[0])], axis=0)


def to_rows(tile):
    return jnp.concatenate(
        [
            jnp.max(jnp.transpose(tile[b * lanes : (b + 1) * lanes, :]), axis=0, keepdims=True)
            for b in range(tile.shape[0] // lanes)
        ],
        axis=0,
    )


def product(left, right):
    return lax.dot_general(left, right, contract_last, preferred_element_type=jnp.float32)


def own_kernel(main, last, out_ref, hold):
    ids = read_ids(main, hold)
    rows = ids.shape[0] * lanes
    blocks = range((first_rows + last.shape[1]) // field)
    columns = columns_of(ids)
    left = features((main, last), blocks, 0, rows)
    steps, per = rows // wide, wide // lanes
    best, tops = [None] * steps, []
    for at in range(steps):
        begin = at * wide
        masked = []
        total = product(left[begin:, :], left[begin : begin + wide, :])
        for h in range(per):
            scores = total[:, h * lanes : (h + 1) * lanes]
            row_ids = ids[at * per + h : at * per + h + 1, :]
            row = lax.broadcasted_iota(jnp.int32, scores.shape, 0)
            column = lax.broadcasted_iota(jnp.int32, scores.shape, 1)
            same = columns[begin:, :] == jnp.where(row_ids < 0, -2.0, row_ids)
            masked.append(jnp.where(same & (row - column != h * lanes), scores, -1.0))
            tops.append(jnp.max(masked[-1], axis=0, keepdims=True))
        both = jnp.maximum(masked[0], masked[1])
        for i in range(at, steps):
            part = both[i * wide - begin : (i + 1) * wide - begin, :]
            best[i] = part if best[i] is None else jnp.maximum(best[i], part)
    out_ref[...] = jnp.maximum(
        to_rows(jnp.concatenate(best, axis=0)), jnp.concatenate(tops, axis=0)
    )


def masked_sums(sums, left_ids, right_ids):
    return jnp.concatenate(
        [
            jnp.where(
                left_ids == jnp.where(right_ids[h : h + 1, :] < 0, -2.0, right_ids[h : h + 1, :]),
                sums[:, h * lanes : (h + 1) * lanes],
                nowhere,
            )
            for h in range(wide // lanes)
        ],
        axis=1,
    )


def start_kernel(spot_ref, main, after, before, near_ref, side_ref, hold):
    low = spot_ref[1] == 1
    ids, after_ids, before_ids = [
        read_ids(ref, hold.at[i]) for i, ref in enumerate((main, after, before))
    ]
    count = ids.shape[0]
    rows = count * lanes
    half = rows // 2
    columns = columns_of(ids)
    right_ids = jnp.where(low, after_ids, before_ids)
    left_ids = jnp.where(low, before_ids[: count // 2, :], after_ids[count // 2 :, :])
    left_columns = columns_of(left_ids)
    blocks = range(early)
    left = features((main,), blocks, 0, rows)
    side_left = jnp.where(
        low, features((before,), blocks, 0, half), features((after,), blocks, half, half)
    )
    per = wide // lanes
    for at in range(rows // wide):
        span, cut = slice(at * wide, (at + 1) * wide), slice(at * per, (at + 1) * per)
        near = features((after,), blocks, at * wide, wide)
        near_ref[:, span] = masked_sums(product(left, near), columns, after_ids[cut, :])
        right = jnp.where(low, near, features((before,), blocks, at * wide, wide))
        side_ref[:, span] = masked_sums(
            product(side_left, right), left_columns, right_ids[cut, :]
        )


def add_block(total, best):
    halves = [total[:, h * lanes : (h + 1) * lanes] for h in range(wide // lanes)]
    for part in halves:
        best = part if best is None else jnp.maximum(best, part)
    return best, [jnp.max(part, axis=0, keepdims=True) for part in halves]


def cross_kernel(
    spot_ref,
    main,
    last,
    after_main,
    after_last,
    before_main,
    before_last,
    near_ref,
    side_ref,
    inside_ref,
    out_ref,
    table,
):
    low = spot_ref[1] == 1
    blocks = inside_ref.shape[0]
    rows = blocks * lanes
    half = rows // 2
    late = range(early, (first_rows + last.shape[1]) // field)
    left, after, before = [
        features(refs, late, 0, rows)
        for refs in ((main, last), (after_main, after_last), (before_main, before_last))
    ]
    side_left = jnp.where(low, before[:half, :], after[half:, :])
    best, far, up, side = None, None, [], []
    for at in range(rows // wide):
        span = slice(at * wide, (at + 1) * wide)
        near = after[span, :]
        right = jnp.where(low, near, before[span, :])
        best, tops = add_block(near_ref[:, span] + product(left, near), best)
        up += tops
        far, tops = add_block(side_ref[:, span] + product(side_left, right), far)
        side += tops
    up, side = jnp.concatenate(up, axis=0), jnp.concatenate(side, axis=0)
    mine = jnp.maximum(to_rows(best), inside_ref[...])
    found = to_rows(far)
    blank = jnp.full(found.shape, -1.0, jnp.float32)
    placed = jnp.where(
        low, jnp.concatenate([found, blank], axis=0), jnp.concatenate([blank, found], axis=0)
    )
    up = jnp.maximum(up, jnp.where(low, side, placed))
    down = jnp.where(low, placed, side)
    count = lanes // field
    steps = (0, 1, places - 1)
    for step, values in enumerate((mine, up, down)):
        for q in range(count):
            turned = values if q == 0 else pltpu.roll(values, lanes - field * q, 1)
            table[step, pl.ds(q, blocks, stride=count), :] = turned
    core, x, y = spot_ref[0], spot_ref[2], spot_ref[3]
    each = places * depth
    across = cores * places

    def found(step, other):
        values = table[step]
        return jnp.where(other == core, values, pltpu.roll(values, lanes - capacity, 1))

    @pl.when(core == 0)
    def _():
        for step, move in enumerate(steps):
            for other in range(cores):
                start = other * places + lax.rem(x + move, places)
                out_ref[pl.ds(start, each, stride=across), :] = found(step, other)

    @pl.when(core == 1)
    def _():
        for step, move in enumerate(steps):
            row = lax.rem(y + move, places) * (depth * across)
            for other in range(cores):
                values = found(step, other)
                for place in range(places):
                    start = row + other * places + place
                    out_ref[pl.ds(start, depth, stride=across), :] = values[
                        place * depth : (place + 1) * depth, :
                    ]


def fetch_kernel(spot_ref, back_ref, plan_ref, out_ref):
    x, y = spot_ref[2], spot_ref[3]
    each = places * depth
    across = cores * places
    even, odd = None, []
    for move in (0, 1, places - 1):
        rows = back_ref[pl.ds(lax.rem(x + move, places), each, stride=across), :]
        even = rows if even is None else jnp.maximum(even, rows)
    for place in range(places):
        total = None
        for move in (0, 1, places - 1):
            start = lax.rem(y + move, places) * (depth * across) + places + place
            rows = back_ref[pl.ds(start, depth, stride=across), :]
            total = rows if total is None else jnp.maximum(total, rows)
        odd.append(total)
    odd = pltpu.roll(jnp.concatenate(odd, axis=0), capacity, 1)
    rest = jnp.where(lax.broadcasted_iota(jnp.int32, even.shape, 1) < capacity, even, odd)
    rest = jnp.where(lax.broadcasted_iota(jnp.int32, even.shape, 1) < field, rest, 0.0)
    rows = plan_ref.shape[1]
    team = lax.broadcasted_iota(jnp.int32, (places * depth, rows), 0)
    onehot = (team == plan_ref[0:1, :]).astype(jnp.bfloat16)
    pieces = []
    for _ in range(3):
        pieces.append(rest.astype(jnp.bfloat16))
        rest = rest - pieces[-1].astype(jnp.float32)
    found = lax.dot_general(
        jnp.concatenate(pieces, axis=0),
        jnp.concatenate([onehot] * 3, axis=0),
        (((0,), (0,)), ((), ())),
        preferred_element_type=jnp.float32,
    )[:field, :]
    lane = lax.broadcasted_iota(jnp.int32, (field, rows), 0)
    out_ref[...] = jnp.sum(jnp.where(lane == plan_ref[1:2, :], found, 0.0), axis=0, keepdims=True)


def send(values, route):
    return lax.ppermute(values, everyone, route)


def trade(values, teams):
    return lax.all_to_all(
        values, everyone, split_axis=0, concat_axis=0, axis_index_groups=teams, tiled=True
    )


def shards(embeddings, owner, cluster):
    rows, width = embeddings.shape
    groups = lax.axis_size("ingest")
    spots = groups * capacity
    blocks = spots // lanes
    each = places * depth
    f32 = jnp.float32
    at, x = lax.axis_index("ingest"), lax.axis_index("span")
    core, y = at % cores, at // (cores * depth)
    low = jnp.where(core == 0, x, y) < places // 2
    spot = jnp.stack([core, low.astype(jnp.int32), x, y]).astype(jnp.int32)
    smem, vmem = pl.BlockSpec(memory_space=pltpu.SMEM), pl.BlockSpec(memory_space=pltpu.VMEM)

    def call(kernel, out_shape, name, *args, scratch=()):
        return pl.pallas_call(
            kernel,
            out_shape=out_shape,
            in_specs=[smem if a is spot else vmem for a in args],
            scratch_shapes=scratch,
            compiler_params=params(),
            name=name,
        )(*args)

    def array(*shape, dtype=jnp.bfloat16):
        return jax.ShapeDtypeStruct(shape, dtype)

    swap = other_core()
    sources = embeddings, owner.reshape(1, rows), cluster.reshape(1, rows)
    others = [send(values, swap) for values in sources]
    total = width // lanes * field
    half, ids, plan = pl.pallas_call(
        functools.partial(place_kernel, groups),
        out_shape=[
            array(each, total // cores, lanes),
            array(each, lanes, dtype=f32),
            array(2, rows, dtype=jnp.int32),
        ],
        in_specs=[smem] + [pl.BlockSpec(memory_space=pltpu.HBM)] * 3,
        scratch_shapes=[pltpu.VMEM(values.shape, values.dtype) for values in sources]
        + [pltpu.SemaphoreType.DMA((3,))],
        compiler_params=params(),
        name="place",
    )(spot, *[pltpu.with_memory_space_constraint(values, pltpu.HBM) for values in sources])
    parts = call(
        functools.partial(pair_kernel, groups),
        [array(each, first_rows + note, lanes), array(each, total - first_rows, lanes)],
        "pair",
        spot,
        *others,
        half,
        ids,
    )
    teams = plane_teams()
    own, after, before = [], [], []
    for part in parts:
        got = trade(part, teams)
        own.append(got)
        before.append(send(got, beside(1)))
        after.append(send(got, beside(-1)))
    held = pltpu.VMEM((each, lanes), f32)
    inside = call(own_kernel, array(blocks, lanes, dtype=f32), "own", *own, scratch=[held])
    near, side = call(
        start_kernel,
        [array(spots, spots, dtype=f32), array(spots // 2, spots, dtype=f32)],
        "start",
        spot,
        own[0],
        after[0],
        before[0],
        scratch=[pltpu.VMEM((3, each, lanes), f32)],
    )
    count = groups * places
    best = call(
        cross_kernel,
        array(count, lanes, dtype=f32),
        "cross",
        spot,
        *own,
        *after,
        *before,
        near,
        side,
        inside,
        scratch=[pltpu.VMEM((3, each, lanes), f32)],
    )
    back = lax.all_to_all(
        best.reshape(count, 1, 1, lanes), everyone, split_axis=0, concat_axis=0, tiled=True
    ).reshape(count, lanes)
    result = call(fetch_kernel, array(1, rows, dtype=f32), "fetch", spot, back, plan)
    return result.reshape(rows)


def solution(mesh):
    placed = (P(("ingest", "span"), None), P(("ingest", "span"), None), P(("ingest", "span")))
    return jax.shard_map(
        shards, mesh=mesh, in_specs=placed, out_specs=P(("ingest", "span")), check_vma=False
    )
```

```python
import functools

import jax
import jax.numpy as jnp
from jax import lax
from jax.experimental import pallas as pl
from jax.experimental.pallas import tpu as pltpu
from jax.sharding import PartitionSpec as P

epsilon = 1e-06
capacity = 16
lanes = 128
wide = 256
cores = 2
places = 4
depth = 8
field = cores * capacity
note = 8
early = 6
first_rows = 208
nowhere = -4.0
core_bits, field_bits = 1, 5
contract_last = (((1,), (1,)), ((), ()))
contract_first = (((1,), (0,)), ((), ()))
everyone = ("ingest", "span")


def params():
    return pltpu.CompilerParams(vmem_limit_bytes=40 * 1024 * 1024)


def device(y, z, core, x):
    return ((y * depth + z) * cores + core) * places + x


def pairs(move):
    found = []
    for y in range(places):
        for z in range(depth):
            for core in range(cores):
                for x in range(places):
                    found.append((device(y, z, core, x), device(*move(y, z, core, x))))
    return found


def other_core():
    return pairs(lambda y, z, core, x: (y, z, 1 - core, x))


def beside(step):
    return pairs(
        lambda y, z, core, x: (y, z, core, (x + step) % places)
        if core == 0
        else ((y + step) % places, z, core, x)
    )


def plane_teams():
    spots, levels = range(places), range(depth)
    return [[device(i, z, 0, x) for i in spots for z in levels] for x in spots] + [
        [device(y, z, 1, i) for i in spots for z in levels] for y in spots
    ]


def rank_rows(owner, groups):
    rows = owner.shape[1]
    belongs = lax.broadcasted_iota(jnp.int32, (groups, rows), 0) == owner
    onehot = belongs.astype(jnp.bfloat16)
    earlier = lax.broadcasted_iota(jnp.int32, (rows, rows), 0) < lax.broadcasted_iota(
        jnp.int32, (rows, rows), 1
    )
    before = lax.dot_general(
        onehot, earlier.astype(jnp.bfloat16), contract_first, preferred_element_type=jnp.float32
    )
    return jnp.sum(jnp.where(belongs, before, 0.0), axis=0, keepdims=True).astype(jnp.int32)


def put_rows(groups, side, spot_ref, emb_ref, owner_ref, cluster_ref):
    core = spot_ref[0]
    owner = owner_ref[...]
    rows = owner.shape[1]
    within = rank_rows(owner, groups)
    slot = jnp.where((owner & (cores - 1)) == core, (owner >> core_bits) * capacity + within, -1)
    room = groups // cores * capacity
    put = (lax.broadcasted_iota(jnp.int32, (room, rows), 0) == slot).astype(jnp.bfloat16)
    values = emb_ref[...].astype(jnp.float32)
    squared = jnp.sum(values * values, axis=1, keepdims=True)
    unit = (values * lax.rsqrt(squared + epsilon)).astype(jnp.bfloat16)

    def placed(start, width):
        return lax.dot_general(
            put,
            unit[:, start : start + width],
            contract_first,
            preferred_element_type=jnp.float32,
        ).astype(jnp.bfloat16)

    team = lax.broadcasted_iota(jnp.int32, (groups // cores, rows), 0)
    here = (team == (owner >> core_bits)) & ((owner & (cores - 1)) == core)
    named = here.astype(jnp.bfloat16) * (cluster_ref[...] + 1).astype(jnp.bfloat16)
    lane = lax.broadcasted_iota(jnp.int32, (lanes, rows), 0)
    into = (lane == within + side * capacity).astype(jnp.bfloat16)
    ids = lax.dot_general(named, into, contract_last, preferred_element_type=jnp.float32)
    return placed, ids, within


def place_kernel(groups, spot_ref, *refs):
    sources, (half_ref, ids_ref, plan_ref), held, done = refs[:3], refs[3:6], refs[6:9], refs[9]
    copies = [
        pltpu.make_async_copy(source, kept, done.at[i])
        for i, (source, kept) in enumerate(zip(sources, held))
    ]
    for copy in copies[::-1]:
        copy.start()
    for copy in copies[::-1]:
        copy.wait()
    placed, ids, within = put_rows(groups, 0, spot_ref, *held)
    teams, count, _ = half_ref.shape
    for start in range(0, count // capacity * lanes, 4 * wide):
        values = placed(start, 4 * wide)
        for shift in range(0, 4 * wide, lanes):
            at = (start + shift) // lanes * capacity
            half_ref[:, at : at + capacity, :] = values[:, shift : shift + lanes].reshape(
                teams, capacity, lanes
            )
    ids_ref[...] = ids
    owner = held[1][...]
    plan_ref[0:1, :] = owner >> core_bits
    plan_ref[1:2, :] = within + (owner & (cores - 1)) * capacity


def pair_kernel(
    groups, spot_ref, emb_ref, owner_ref, cluster_ref, half_ref, ids_ref, main_ref, last_ref
):
    placed, ids, _ = put_rows(groups, 1, spot_ref, emb_ref, owner_ref, cluster_ref)
    teams, count, _ = half_ref.shape
    border = main_ref.shape[1] - note

    def store(at, values):
        if at < border:
            main_ref[:, at : at + capacity, :] = values
        else:
            last_ref[:, at - border : at - border + capacity, :] = values

    for start in range(0, count // capacity * lanes, 4 * wide):
        values = placed(start, 4 * wide)
        for shift in range(0, 4 * wide, lanes):
            block = (start + shift) // lanes
            store(block * field, half_ref[:, block * capacity : (block + 1) * capacity, :])
            store(
                block * field + capacity,
                values[:, shift : shift + lanes].reshape(teams, capacity, lanes),
            )
    ids = (ids + ids_ref[...] - 1.0).astype(jnp.bfloat16)
    main_ref[:, border:, :] = jnp.broadcast_to(
        ids[:, None, :], (teams, note, lanes)
    )


def read_ids(ref, hold):
    count = lanes // field
    blocks = ref.shape[0] // count
    hold[...] = jnp.max(ref[:, ref.shape[1] - note :, :].astype(jnp.float32), axis=1)
    lane = lax.broadcasted_iota(jnp.int32, (blocks, lanes), 1)
    total = hold[pl.ds(0, blocks, stride=count), :]
    for q in range(1, count):
        piece = pltpu.roll(hold[pl.ds(q, blocks, stride=count), :], field * q, 1)
        total = jnp.where(lane >> field_bits == q, piece, total)
    return total


def features(refs, blocks, start, count):
    teams = slice(start // field, (start + count) // field)
    found = []
    for block in blocks:
        low, high = block * field, (block + 1) * field
        parts = []
        if low < first_rows:
            parts.append(refs[0][teams, low : min(high, first_rows), :])
        if high > first_rows:
            parts.append(refs[1][teams, max(low, first_rows) - first_rows : high - first_rows, :])
        piece = parts[0] if len(parts) == 1 else jnp.concatenate(parts, axis=1)
        found.append(piece.reshape(count, lanes))
    return jnp.concatenate(found, axis=1)


def to_column(row):
    return jnp.transpose(jnp.broadcast_to(row, (lanes, lanes)))


def columns_of(ids):
    return jnp.concatenate([to_column(ids[b : b + 1, :]) for b in range(ids.shape[0])], axis=0)


def to_rows(tile):
    return jnp.concatenate(
        [
            jnp.max(jnp.transpose(tile[b * lanes : (b + 1) * lanes, :]), axis=0, keepdims=True)
            for b in range(tile.shape[0] // lanes)
        ],
        axis=0,
    )


def product(left, right):
    return lax.dot_general(left, right, contract_last, preferred_element_type=jnp.float32)


def own_kernel(main, last, plan_ref, out_ref, onehot_ref, pick_ref, hold):
    team = lax.broadcasted_iota(jnp.int32, pick_ref.shape, 0)
    onehot = (team == plan_ref[0:1, :]).astype(jnp.bfloat16)
    onehot_ref[...] = jnp.concatenate([onehot] * 3, axis=0)
    pick_ref[...] = jnp.where(team == plan_ref[1:2, :], 1.0, 0.0)
    ids = read_ids(main, hold)
    rows = ids.shape[0] * lanes
    blocks = range((first_rows + last.shape[1]) // field)
    columns = columns_of(ids)
    left = features((main, last), blocks, 0, rows)
    steps, per = rows // wide, wide // lanes
    best, tops = [None] * steps, []
    for at in range(steps):
        begin = at * wide
        masked = []
        total = product(left[begin:, :], left[begin : begin + wide, :])
        for h in range(per):
            scores = total[:, h * lanes : (h + 1) * lanes]
            row_ids = ids[at * per + h : at * per + h + 1, :]
            row = lax.broadcasted_iota(jnp.int32, scores.shape, 0)
            column = lax.broadcasted_iota(jnp.int32, scores.shape, 1)
            same = columns[begin:, :] == jnp.where(row_ids < 0, -2.0, row_ids)
            masked.append(jnp.where(same & (row - column != h * lanes), scores, -1.0))
            tops.append(jnp.max(masked[-1], axis=0, keepdims=True))
        both = jnp.maximum(masked[0], masked[1])
        for i in range(at, steps):
            part = both[i * wide - begin : (i + 1) * wide - begin, :]
            best[i] = part if best[i] is None else jnp.maximum(best[i], part)
    out_ref[...] = jnp.maximum(
        to_rows(jnp.concatenate(best, axis=0)), jnp.concatenate(tops, axis=0)
    )


def masked_sums(sums, left_ids, right_ids):
    return jnp.concatenate(
        [
            jnp.where(
                left_ids == jnp.where(right_ids[h : h + 1, :] < 0, -2.0, right_ids[h : h + 1, :]),
                sums[:, h * lanes : (h + 1) * lanes],
                nowhere,
            )
            for h in range(wide // lanes)
        ],
        axis=1,
    )


def start_kernel(spot_ref, main, after, before, near_ref, side_ref, hold):
    low = spot_ref[1] == 1
    ids, after_ids, before_ids = [
        read_ids(ref, hold.at[i]) for i, ref in enumerate((main, after, before))
    ]
    count = ids.shape[0]
    rows = count * lanes
    half = rows // 2
    columns = columns_of(ids)
    right_ids = jnp.where(low, after_ids, before_ids)
    left_ids = jnp.where(low, before_ids[: count // 2, :], after_ids[count // 2 :, :])
    left_columns = columns_of(left_ids)
    blocks = range(early)
    left = features((main,), blocks, 0, rows)
    side_left = jnp.where(
        low, features((before,), blocks, 0, half), features((after,), blocks, half, half)
    )
    per = wide // lanes
    for at in range(rows // wide):
        span, cut = slice(at * wide, (at + 1) * wide), slice(at * per, (at + 1) * per)
        near = features((after,), blocks, at * wide, wide)
        near_ref[:, span] = masked_sums(product(left, near), columns, after_ids[cut, :])
        right = jnp.where(low, near, features((before,), blocks, at * wide, wide))
        side_ref[:, span] = masked_sums(
            product(side_left, right), left_columns, right_ids[cut, :]
        )


def add_block(total, best):
    halves = [total[:, h * lanes : (h + 1) * lanes] for h in range(wide // lanes)]
    for part in halves:
        best = part if best is None else jnp.maximum(best, part)
    return best, [jnp.max(part, axis=0, keepdims=True) for part in halves]


def cross_kernel(
    spot_ref,
    main,
    last,
    after_main,
    after_last,
    before_main,
    before_last,
    near_ref,
    side_ref,
    inside_ref,
    out_ref,
    table,
):
    low = spot_ref[1] == 1
    blocks = inside_ref.shape[0]
    rows = blocks * lanes
    half = rows // 2
    late = range(early, (first_rows + last.shape[1]) // field)
    left, after, before = [
        features(refs, late, 0, rows)
        for refs in ((main, last), (after_main, after_last), (before_main, before_last))
    ]
    side_left = jnp.where(low, before[:half, :], after[half:, :])
    best, far, up, side = None, None, [], []
    for at in range(rows // wide):
        span = slice(at * wide, (at + 1) * wide)
        near = after[span, :]
        right = jnp.where(low, near, before[span, :])
        best, tops = add_block(near_ref[:, span] + product(left, near), best)
        up += tops
        far, tops = add_block(side_ref[:, span] + product(side_left, right), far)
        side += tops
    up, side = jnp.concatenate(up, axis=0), jnp.concatenate(side, axis=0)
    mine = jnp.maximum(to_rows(best), inside_ref[...])
    found = to_rows(far)
    blank = jnp.full(found.shape, -1.0, jnp.float32)
    placed = jnp.where(
        low, jnp.concatenate([found, blank], axis=0), jnp.concatenate([blank, found], axis=0)
    )
    up = jnp.maximum(up, jnp.where(low, side, placed))
    down = jnp.where(low, placed, side)
    count = lanes // field
    steps = (0, 1, places - 1)
    for step, values in enumerate((mine, up, down)):
        for q in range(count):
            turned = values if q == 0 else pltpu.roll(values, lanes - field * q, 1)
            table[step, pl.ds(q, blocks, stride=count), :] = turned
    core, x, y = spot_ref[0], spot_ref[2], spot_ref[3]
    each = places * depth
    across = cores * places

    def found(step, other):
        values = table[step]
        return jnp.where(other == core, values, pltpu.roll(values, lanes - capacity, 1))

    @pl.when(core == 0)
    def _():
        for step, move in enumerate(steps):
            for other in range(cores):
                start = other * places + lax.rem(x + move, places)
                out_ref[pl.ds(start, each, stride=across), :] = found(step, other)

    @pl.when(core == 1)
    def _():
        for step, move in enumerate(steps):
            row = lax.rem(y + move, places) * (depth * across)
            for other in range(cores):
                values = found(step, other)
                for place in range(places):
                    start = row + other * places + place
                    out_ref[pl.ds(start, depth, stride=across), :] = values[
                        place * depth : (place + 1) * depth, :
                    ]


def fetch_kernel(spot_ref, back_ref, onehot_ref, pick_ref, out_ref):
    x, y = spot_ref[2], spot_ref[3]
    each = places * depth
    across = cores * places
    even, odd = None, []
    for move in (0, 1, places - 1):
        rows = back_ref[pl.ds(lax.rem(x + move, places), each, stride=across), :]
        even = rows if even is None else jnp.maximum(even, rows)
    for place in range(places):
        total = None
        for move in (0, 1, places - 1):
            start = lax.rem(y + move, places) * (depth * across) + places + place
            rows = back_ref[pl.ds(start, depth, stride=across), :]
            total = rows if total is None else jnp.maximum(total, rows)
        odd.append(total)
    odd = pltpu.roll(jnp.concatenate(odd, axis=0), capacity, 1)
    rest = jnp.where(lax.broadcasted_iota(jnp.int32, even.shape, 1) < capacity, even, odd)
    rest = jnp.where(lax.broadcasted_iota(jnp.int32, even.shape, 1) < field, rest, 0.0)
    pieces = []
    for _ in range(3):
        pieces.append(rest.astype(jnp.bfloat16))
        rest = rest - pieces[-1].astype(jnp.float32)
    found = lax.dot_general(
        jnp.concatenate(pieces, axis=0),
        onehot_ref[...],
        (((0,), (0,)), ((), ())),
        preferred_element_type=jnp.float32,
    )[:field, :]
    out_ref[...] = jnp.sum(jnp.where(pick_ref[...] > 0, found, 0.0), axis=0, keepdims=True)


def send(values, route):
    return lax.ppermute(values, everyone, route)


def trade(values, teams):
    return lax.all_to_all(
        values, everyone, split_axis=0, concat_axis=0, axis_index_groups=teams, tiled=True
    )


def shards(embeddings, owner, cluster):
    rows, width = embeddings.shape
    groups = lax.axis_size("ingest")
    spots = groups * capacity
    blocks = spots // lanes
    each = places * depth
    f32 = jnp.float32
    at, x = lax.axis_index("ingest"), lax.axis_index("span")
    core, y = at % cores, at // (cores * depth)
    low = jnp.where(core == 0, x, y) < places // 2
    spot = jnp.stack([core, low.astype(jnp.int32), x, y]).astype(jnp.int32)
    smem, vmem = pl.BlockSpec(memory_space=pltpu.SMEM), pl.BlockSpec(memory_space=pltpu.VMEM)

    def call(kernel, out_shape, name, *args, scratch=()):
        return pl.pallas_call(
            kernel,
            out_shape=out_shape,
            in_specs=[smem if a is spot else vmem for a in args],
            scratch_shapes=scratch,
            compiler_params=params(),
            name=name,
        )(*args)

    def array(*shape, dtype=jnp.bfloat16):
        return jax.ShapeDtypeStruct(shape, dtype)

    swap = other_core()
    sources = embeddings, owner.reshape(1, rows), cluster.reshape(1, rows)
    others = [send(values, swap) for values in sources]
    total = width // lanes * field
    half, ids, plan = pl.pallas_call(
        functools.partial(place_kernel, groups),
        out_shape=[
            array(each, total // cores, lanes),
            array(each, lanes, dtype=f32),
            array(2, rows, dtype=jnp.int32),
        ],
        in_specs=[smem] + [pl.BlockSpec(memory_space=pltpu.HBM)] * 3,
        scratch_shapes=[pltpu.VMEM(values.shape, values.dtype) for values in sources]
        + [pltpu.SemaphoreType.DMA((3,))],
        compiler_params=params(),
        name="place",
    )(spot, *[pltpu.with_memory_space_constraint(values, pltpu.HBM) for values in sources])
    parts = call(
        functools.partial(pair_kernel, groups),
        [array(each, first_rows + note, lanes), array(each, total - first_rows, lanes)],
        "pair",
        spot,
        *others,
        half,
        ids,
    )
    teams = plane_teams()
    own, after, before = [], [], []
    for part in parts:
        got = trade(part, teams)
        own.append(got)
        before.append(send(got, beside(1)))
        after.append(send(got, beside(-1)))
    held = pltpu.VMEM((each, lanes), f32)
    inside, onehot, pick = call(
        own_kernel,
        [array(blocks, lanes, dtype=f32), array(3 * each, rows), array(each, rows, dtype=f32)],
        "own",
        *own,
        plan,
        scratch=[held],
    )
    near, side = call(
        start_kernel,
        [array(spots, spots, dtype=f32), array(spots // 2, spots, dtype=f32)],
        "start",
        spot,
        own[0],
        after[0],
        before[0],
        scratch=[pltpu.VMEM((3, each, lanes), f32)],
    )
    count = groups * places
    best = call(
        cross_kernel,
        array(count, lanes, dtype=f32),
        "cross",
        spot,
        *own,
        *after,
        *before,
        near,
        side,
        inside,
        scratch=[pltpu.VMEM((3, each, lanes), f32)],
    )
    back = lax.all_to_all(
        best.reshape(count, 1, 1, lanes), everyone, split_axis=0, concat_axis=0, tiled=True
    ).reshape(count, lanes)
    result = call(fetch_kernel, array(1, rows, dtype=f32), "fetch", spot, back, onehot, pick)
    return result.reshape(rows)


def solution(mesh):
    placed = (P(("ingest", "span"), None), P(("ingest", "span"), None), P(("ingest", "span")))
    return jax.shard_map(
        shards, mesh=mesh, in_specs=placed, out_specs=P(("ingest", "span")), check_vma=False
    )
```

```python
import functools

import jax
import jax.numpy as jnp
from jax import lax
from jax.experimental import pallas as pl
from jax.experimental.pallas import tpu as pltpu
from jax.sharding import PartitionSpec as P

epsilon = 1e-06
capacity = 16
lanes = 128
wide = 512
cores = 2
places = 4
depth = 8
field = cores * capacity
note = 8
early = 6
first_rows = 208
nowhere = -4.0
core_bits, field_bits = 1, 5
contract_last = (((1,), (1,)), ((), ()))
contract_first = (((1,), (0,)), ((), ()))
everyone = ("ingest", "span")


def params():
    return pltpu.CompilerParams(vmem_limit_bytes=40 * 1024 * 1024)


def device(y, z, core, x):
    return ((y * depth + z) * cores + core) * places + x


def pairs(move):
    found = []
    for y in range(places):
        for z in range(depth):
            for core in range(cores):
                for x in range(places):
                    found.append((device(y, z, core, x), device(*move(y, z, core, x))))
    return found


def other_core():
    return pairs(lambda y, z, core, x: (y, z, 1 - core, x))


def beside(step):
    return pairs(
        lambda y, z, core, x: (y, z, core, (x + step) % places)
        if core == 0
        else ((y + step) % places, z, core, x)
    )


def plane_teams():
    spots, levels = range(places), range(depth)
    return [[device(i, z, 0, x) for i in spots for z in levels] for x in spots] + [
        [device(y, z, 1, i) for i in spots for z in levels] for y in spots
    ]


def rank_rows(owner, groups):
    rows = owner.shape[1]
    belongs = lax.broadcasted_iota(jnp.int32, (groups, rows), 0) == owner
    onehot = belongs.astype(jnp.bfloat16)
    earlier = lax.broadcasted_iota(jnp.int32, (rows, rows), 0) < lax.broadcasted_iota(
        jnp.int32, (rows, rows), 1
    )
    before = lax.dot_general(
        onehot, earlier.astype(jnp.bfloat16), contract_first, preferred_element_type=jnp.float32
    )
    return jnp.sum(jnp.where(belongs, before, 0.0), axis=0, keepdims=True).astype(jnp.int32)


def put_rows(groups, side, spot_ref, emb_ref, owner_ref, cluster_ref):
    core = spot_ref[0]
    owner = owner_ref[...]
    rows = owner.shape[1]
    within = rank_rows(owner, groups)
    slot = jnp.where((owner & (cores - 1)) == core, (owner >> core_bits) * capacity + within, -1)
    room = groups // cores * capacity
    put = (lax.broadcasted_iota(jnp.int32, (room, rows), 0) == slot).astype(jnp.bfloat16)
    values = emb_ref[...].astype(jnp.float32)
    squared = jnp.sum(values * values, axis=1, keepdims=True)
    unit = (values * lax.rsqrt(squared + epsilon)).astype(jnp.bfloat16)

    def placed(start, width):
        return lax.dot_general(
            put,
            unit[:, start : start + width],
            contract_first,
            preferred_element_type=jnp.float32,
        ).astype(jnp.bfloat16)

    team = lax.broadcasted_iota(jnp.int32, (groups // cores, rows), 0)
    here = (team == (owner >> core_bits)) & ((owner & (cores - 1)) == core)
    named = here.astype(jnp.bfloat16) * (cluster_ref[...] + 1).astype(jnp.bfloat16)
    lane = lax.broadcasted_iota(jnp.int32, (lanes, rows), 0)
    into = (lane == within + side * capacity).astype(jnp.bfloat16)
    ids = lax.dot_general(named, into, contract_last, preferred_element_type=jnp.float32)
    return placed, ids, within


def place_kernel(groups, spot_ref, *refs):
    sources, (half_ref, ids_ref, plan_ref), held, done = refs[:3], refs[3:6], refs[6:9], refs[9]
    copies = [
        pltpu.make_async_copy(source, kept, done.at[i])
        for i, (source, kept) in enumerate(zip(sources, held))
    ]
    for copy in copies[::-1]:
        copy.start()
    for copy in copies[::-1]:
        copy.wait()
    placed, ids, within = put_rows(groups, 0, spot_ref, *held)
    teams, count, _ = half_ref.shape
    for start in range(0, count // capacity * lanes, 2 * wide):
        values = placed(start, 2 * wide)
        for shift in range(0, 2 * wide, lanes):
            at = (start + shift) // lanes * capacity
            half_ref[:, at : at + capacity, :] = values[:, shift : shift + lanes].reshape(
                teams, capacity, lanes
            )
    ids_ref[...] = ids
    owner = held[1][...]
    plan_ref[0:1, :] = owner >> core_bits
    plan_ref[1:2, :] = within + (owner & (cores - 1)) * capacity


def pair_kernel(
    groups, spot_ref, emb_ref, owner_ref, cluster_ref, half_ref, ids_ref, main_ref, last_ref
):
    placed, ids, _ = put_rows(groups, 1, spot_ref, emb_ref, owner_ref, cluster_ref)
    teams, count, _ = half_ref.shape
    border = main_ref.shape[1] - note

    def store(at, values):
        if at < border:
            main_ref[:, at : at + capacity, :] = values
        else:
            last_ref[:, at - border : at - border + capacity, :] = values

    for start in range(0, count // capacity * lanes, 2 * wide):
        values = placed(start, 2 * wide)
        for shift in range(0, 2 * wide, lanes):
            block = (start + shift) // lanes
            store(block * field, half_ref[:, block * capacity : (block + 1) * capacity, :])
            store(
                block * field + capacity,
                values[:, shift : shift + lanes].reshape(teams, capacity, lanes),
            )
    ids = (ids + ids_ref[...] - 1.0).astype(jnp.bfloat16)
    main_ref[:, border:, :] = jnp.broadcast_to(
        ids[:, None, :], (teams, note, lanes)
    )


def read_ids(ref, hold):
    count = lanes // field
    blocks = ref.shape[0] // count
    hold[...] = jnp.max(ref[:, ref.shape[1] - note :, :].astype(jnp.float32), axis=1)
    lane = lax.broadcasted_iota(jnp.int32, (blocks, lanes), 1)
    total = hold[pl.ds(0, blocks, stride=count), :]
    for q in range(1, count):
        piece = pltpu.roll(hold[pl.ds(q, blocks, stride=count), :], field * q, 1)
        total = jnp.where(lane >> field_bits == q, piece, total)
    return total


def features(refs, blocks, start, count):
    teams = slice(start // field, (start + count) // field)
    found = []
    for block in blocks:
        low, high = block * field, (block + 1) * field
        parts = []
        if low < first_rows:
            parts.append(refs[0][teams, low : min(high, first_rows), :])
        if high > first_rows:
            parts.append(refs[1][teams, max(low, first_rows) - first_rows : high - first_rows, :])
        piece = parts[0] if len(parts) == 1 else jnp.concatenate(parts, axis=1)
        found.append(piece.reshape(count, lanes))
    return jnp.concatenate(found, axis=1)


def to_column(row):
    return jnp.transpose(jnp.broadcast_to(row, (lanes, lanes)))


def columns_of(ids):
    return jnp.concatenate([to_column(ids[b : b + 1, :]) for b in range(ids.shape[0])], axis=0)


def to_rows(tile):
    return jnp.concatenate(
        [
            jnp.max(jnp.transpose(tile[b * lanes : (b + 1) * lanes, :]), axis=0, keepdims=True)
            for b in range(tile.shape[0] // lanes)
        ],
        axis=0,
    )


def product(left, right):
    return lax.dot_general(left, right, contract_last, preferred_element_type=jnp.float32)


def own_kernel(main, last, plan_ref, out_ref, onehot_ref, pick_ref, hold):
    team = lax.broadcasted_iota(jnp.int32, pick_ref.shape, 0)
    onehot = (team == plan_ref[0:1, :]).astype(jnp.bfloat16)
    onehot_ref[...] = jnp.concatenate([onehot] * 3, axis=0)
    pick_ref[...] = jnp.where(team == plan_ref[1:2, :], 1.0, 0.0)
    ids = read_ids(main, hold)
    rows = ids.shape[0] * lanes
    blocks = range((first_rows + last.shape[1]) // field)
    columns = columns_of(ids)
    left = features((main, last), blocks, 0, rows)
    steps, per = rows // wide, wide // lanes
    best, tops = [None] * steps, []
    for at in range(steps):
        begin = at * wide
        masked = []
        total = product(left[begin:, :], left[begin : begin + wide, :])
        for h in range(per):
            scores = total[:, h * lanes : (h + 1) * lanes]
            row_ids = ids[at * per + h : at * per + h + 1, :]
            row = lax.broadcasted_iota(jnp.int32, scores.shape, 0)
            column = lax.broadcasted_iota(jnp.int32, scores.shape, 1)
            same = columns[begin:, :] == jnp.where(row_ids < 0, -2.0, row_ids)
            masked.append(jnp.where(same & (row - column != h * lanes), scores, -1.0))
            tops.append(jnp.max(masked[-1], axis=0, keepdims=True))
        both = functools.reduce(jnp.maximum, masked)
        for i in range(at, steps):
            part = both[i * wide - begin : (i + 1) * wide - begin, :]
            best[i] = part if best[i] is None else jnp.maximum(best[i], part)
    out_ref[...] = jnp.maximum(
        to_rows(jnp.concatenate(best, axis=0)), jnp.concatenate(tops, axis=0)
    )


def masked_sums(sums, left_ids, right_ids):
    return jnp.concatenate(
        [
            jnp.where(
                left_ids == jnp.where(right_ids[h : h + 1, :] < 0, -2.0, right_ids[h : h + 1, :]),
                sums[:, h * lanes : (h + 1) * lanes],
                nowhere,
            )
            for h in range(wide // lanes)
        ],
        axis=1,
    )


def start_kernel(spot_ref, main, after, before, near_ref, side_ref, hold):
    low = spot_ref[1] == 1
    ids, after_ids, before_ids = [
        read_ids(ref, hold.at[i]) for i, ref in enumerate((main, after, before))
    ]
    count = ids.shape[0]
    rows = count * lanes
    half = rows // 2
    columns = columns_of(ids)
    right_ids = jnp.where(low, after_ids, before_ids)
    left_ids = jnp.where(low, before_ids[: count // 2, :], after_ids[count // 2 :, :])
    left_columns = columns_of(left_ids)
    blocks = range(early)
    left = features((main,), blocks, 0, rows)
    side_left = jnp.where(
        low, features((before,), blocks, 0, half), features((after,), blocks, half, half)
    )
    per = wide // lanes
    for at in range(rows // wide):
        span, cut = slice(at * wide, (at + 1) * wide), slice(at * per, (at + 1) * per)
        near = features((after,), blocks, at * wide, wide)
        near_ref[:, span] = masked_sums(product(left, near), columns, after_ids[cut, :])
        right = jnp.where(low, near, features((before,), blocks, at * wide, wide))
        side_ref[:, span] = masked_sums(
            product(side_left, right), left_columns, right_ids[cut, :]
        )


def add_block(total, best):
    halves = [total[:, h * lanes : (h + 1) * lanes] for h in range(wide // lanes)]
    for part in halves:
        best = part if best is None else jnp.maximum(best, part)
    return best, [jnp.max(part, axis=0, keepdims=True) for part in halves]


def cross_kernel(
    spot_ref,
    main,
    last,
    after_main,
    after_last,
    before_main,
    before_last,
    near_ref,
    side_ref,
    inside_ref,
    out_ref,
    table,
):
    low = spot_ref[1] == 1
    blocks = inside_ref.shape[0]
    rows = blocks * lanes
    half = rows // 2
    late = range(early, (first_rows + last.shape[1]) // field)
    left, after, before = [
        features(refs, late, 0, rows)
        for refs in ((main, last), (after_main, after_last), (before_main, before_last))
    ]
    side_left = jnp.where(low, before[:half, :], after[half:, :])
    best, far, up, side = None, None, [], []
    for at in range(rows // wide):
        span = slice(at * wide, (at + 1) * wide)
        near = after[span, :]
        right = jnp.where(low, near, before[span, :])
        best, tops = add_block(near_ref[:, span] + product(left, near), best)
        up += tops
        far, tops = add_block(side_ref[:, span] + product(side_left, right), far)
        side += tops
    up, side = jnp.concatenate(up, axis=0), jnp.concatenate(side, axis=0)
    mine = jnp.maximum(to_rows(best), inside_ref[...])
    found = to_rows(far)
    blank = jnp.full(found.shape, -1.0, jnp.float32)
    placed = jnp.where(
        low, jnp.concatenate([found, blank], axis=0), jnp.concatenate([blank, found], axis=0)
    )
    up = jnp.maximum(up, jnp.where(low, side, placed))
    down = jnp.where(low, placed, side)
    count = lanes // field
    steps = (0, 1, places - 1)
    for step, values in enumerate((mine, up, down)):
        for q in range(count):
            turned = values if q == 0 else pltpu.roll(values, lanes - field * q, 1)
            table[step, pl.ds(q, blocks, stride=count), :] = turned
    core, x, y = spot_ref[0], spot_ref[2], spot_ref[3]
    each = places * depth
    across = cores * places

    def found(step, other):
        values = table[step]
        return jnp.where(other == core, values, pltpu.roll(values, lanes - capacity, 1))

    @pl.when(core == 0)
    def _():
        for step, move in enumerate(steps):
            for other in range(cores):
                start = other * places + lax.rem(x + move, places)
                out_ref[pl.ds(start, each, stride=across), :] = found(step, other)

    @pl.when(core == 1)
    def _():
        for step, move in enumerate(steps):
            row = lax.rem(y + move, places) * (depth * across)
            for other in range(cores):
                values = found(step, other)
                for place in range(places):
                    start = row + other * places + place
                    out_ref[pl.ds(start, depth, stride=across), :] = values[
                        place * depth : (place + 1) * depth, :
                    ]


def fetch_kernel(spot_ref, back_ref, onehot_ref, pick_ref, out_ref):
    x, y = spot_ref[2], spot_ref[3]
    each = places * depth
    across = cores * places
    even, odd = None, []
    for move in (0, 1, places - 1):
        rows = back_ref[pl.ds(lax.rem(x + move, places), each, stride=across), :]
        even = rows if even is None else jnp.maximum(even, rows)
    for place in range(places):
        total = None
        for move in (0, 1, places - 1):
            start = lax.rem(y + move, places) * (depth * across) + places + place
            rows = back_ref[pl.ds(start, depth, stride=across), :]
            total = rows if total is None else jnp.maximum(total, rows)
        odd.append(total)
    odd = pltpu.roll(jnp.concatenate(odd, axis=0), capacity, 1)
    rest = jnp.where(lax.broadcasted_iota(jnp.int32, even.shape, 1) < capacity, even, odd)
    rest = jnp.where(lax.broadcasted_iota(jnp.int32, even.shape, 1) < field, rest, 0.0)
    pieces = []
    for _ in range(3):
        pieces.append(rest.astype(jnp.bfloat16))
        rest = rest - pieces[-1].astype(jnp.float32)
    found = lax.dot_general(
        jnp.concatenate(pieces, axis=0),
        onehot_ref[...],
        (((0,), (0,)), ((), ())),
        preferred_element_type=jnp.float32,
    )[:field, :]
    out_ref[...] = jnp.sum(jnp.where(pick_ref[...] > 0, found, 0.0), axis=0, keepdims=True)


def send(values, route):
    return lax.ppermute(values, everyone, route)


def trade(values, teams):
    return lax.all_to_all(
        values, everyone, split_axis=0, concat_axis=0, axis_index_groups=teams, tiled=True
    )


def shards(embeddings, owner, cluster):
    rows, width = embeddings.shape
    groups = lax.axis_size("ingest")
    spots = groups * capacity
    blocks = spots // lanes
    each = places * depth
    f32 = jnp.float32
    at, x = lax.axis_index("ingest"), lax.axis_index("span")
    core, y = at % cores, at // (cores * depth)
    low = jnp.where(core == 0, x, y) < places // 2
    spot = jnp.stack([core, low.astype(jnp.int32), x, y]).astype(jnp.int32)
    smem, vmem = pl.BlockSpec(memory_space=pltpu.SMEM), pl.BlockSpec(memory_space=pltpu.VMEM)

    def call(kernel, out_shape, name, *args, scratch=()):
        return pl.pallas_call(
            kernel,
            out_shape=out_shape,
            in_specs=[smem if a is spot else vmem for a in args],
            scratch_shapes=scratch,
            compiler_params=params(),
            name=name,
        )(*args)

    def array(*shape, dtype=jnp.bfloat16):
        return jax.ShapeDtypeStruct(shape, dtype)

    swap = other_core()
    sources = embeddings, owner.reshape(1, rows), cluster.reshape(1, rows)
    others = [send(values, swap) for values in sources]
    total = width // lanes * field
    half, ids, plan = pl.pallas_call(
        functools.partial(place_kernel, groups),
        out_shape=[
            array(each, total // cores, lanes),
            array(each, lanes, dtype=f32),
            array(2, rows, dtype=jnp.int32),
        ],
        in_specs=[smem] + [pl.BlockSpec(memory_space=pltpu.HBM)] * 3,
        scratch_shapes=[pltpu.VMEM(values.shape, values.dtype) for values in sources]
        + [pltpu.SemaphoreType.DMA((3,))],
        compiler_params=params(),
        name="place",
    )(spot, *[pltpu.with_memory_space_constraint(values, pltpu.HBM) for values in sources])
    parts = call(
        functools.partial(pair_kernel, groups),
        [array(each, first_rows + note, lanes), array(each, total - first_rows, lanes)],
        "pair",
        spot,
        *others,
        half,
        ids,
    )
    teams = plane_teams()
    own, after, before = [], [], []
    for part in parts:
        got = trade(part, teams)
        own.append(got)
        before.append(send(got, beside(1)))
        after.append(send(got, beside(-1)))
    held = pltpu.VMEM((each, lanes), f32)
    inside, onehot, pick = call(
        own_kernel,
        [array(blocks, lanes, dtype=f32), array(3 * each, rows), array(each, rows, dtype=f32)],
        "own",
        *own,
        plan,
        scratch=[held],
    )
    near, side = call(
        start_kernel,
        [array(spots, spots, dtype=f32), array(spots // 2, spots, dtype=f32)],
        "start",
        spot,
        own[0],
        after[0],
        before[0],
        scratch=[pltpu.VMEM((3, each, lanes), f32)],
    )
    count = groups * places
    best = call(
        cross_kernel,
        array(count, lanes, dtype=f32),
        "cross",
        spot,
        *own,
        *after,
        *before,
        near,
        side,
        inside,
        scratch=[pltpu.VMEM((3, each, lanes), f32)],
    )
    back = lax.all_to_all(
        best.reshape(count, 1, 1, lanes), everyone, split_axis=0, concat_axis=0, tiled=True
    ).reshape(count, lanes)
    result = call(fetch_kernel, array(1, rows, dtype=f32), "fetch", spot, back, onehot, pick)
    return result.reshape(rows)


def solution(mesh):
    placed = (P(("ingest", "span"), None), P(("ingest", "span"), None), P(("ingest", "span")))
    return jax.shard_map(
        shards, mesh=mesh, in_specs=placed, out_specs=P(("ingest", "span")), check_vma=False
    )
```

```python
import functools

import jax
import jax.numpy as jnp
from jax import lax
from jax.experimental import pallas as pl
from jax.experimental.pallas import tpu as pltpu
from jax.sharding import PartitionSpec as P

epsilon = 1e-06
capacity = 16
lanes = 128
wide = 256
cores = 2
places = 4
depth = 8
field = cores * capacity
note = 8
early = 6
first_rows = 208
nowhere = -4.0
core_bits, field_bits = 1, 5
contract_last = (((1,), (1,)), ((), ()))
contract_first = (((1,), (0,)), ((), ()))
everyone = ("ingest", "span")


def params():
    return pltpu.CompilerParams(vmem_limit_bytes=40 * 1024 * 1024)


def device(y, z, core, x):
    return ((y * depth + z) * cores + core) * places + x


def pairs(move):
    found = []
    for y in range(places):
        for z in range(depth):
            for core in range(cores):
                for x in range(places):
                    found.append((device(y, z, core, x), device(*move(y, z, core, x))))
    return found


def other_core():
    return pairs(lambda y, z, core, x: (y, z, 1 - core, x))


def beside(step):
    return pairs(
        lambda y, z, core, x: (y, z, core, (x + step) % places)
        if core == 0
        else ((y + step) % places, z, core, x)
    )


def plane_teams():
    spots, levels = range(places), range(depth)
    return [[device(i, z, 0, x) for i in spots for z in levels] for x in spots] + [
        [device(y, z, 1, i) for i in spots for z in levels] for y in spots
    ]


def rank_rows(owner, groups):
    rows = owner.shape[1]
    belongs = lax.broadcasted_iota(jnp.int32, (groups, rows), 0) == owner
    onehot = belongs.astype(jnp.bfloat16)
    earlier = lax.broadcasted_iota(jnp.int32, (rows, rows), 0) < lax.broadcasted_iota(
        jnp.int32, (rows, rows), 1
    )
    before = lax.dot_general(
        onehot, earlier.astype(jnp.bfloat16), contract_first, preferred_element_type=jnp.float32
    )
    return jnp.sum(jnp.where(belongs, before, 0.0), axis=0, keepdims=True).astype(jnp.int32)


def put_rows(groups, side, spot_ref, emb_ref, owner_ref, cluster_ref):
    core = spot_ref[0]
    owner = owner_ref[...]
    rows = owner.shape[1]
    within = rank_rows(owner, groups)
    slot = jnp.where((owner & (cores - 1)) == core, (owner >> core_bits) * capacity + within, -1)
    room = groups // cores * capacity
    put = (lax.broadcasted_iota(jnp.int32, (room, rows), 0) == slot).astype(jnp.bfloat16)
    values = emb_ref[...].astype(jnp.float32)
    squared = jnp.sum(values * values, axis=1, keepdims=True)
    unit = (values * lax.rsqrt(squared + epsilon)).astype(jnp.bfloat16)

    def placed(start, width):
        return lax.dot_general(
            put,
            unit[:, start : start + width],
            contract_first,
            preferred_element_type=jnp.float32,
        ).astype(jnp.bfloat16)

    team = lax.broadcasted_iota(jnp.int32, (groups // cores, rows), 0)
    here = (team == (owner >> core_bits)) & ((owner & (cores - 1)) == core)
    named = here.astype(jnp.bfloat16) * (cluster_ref[...] + 1).astype(jnp.bfloat16)
    lane = lax.broadcasted_iota(jnp.int32, (lanes, rows), 0)
    into = (lane == within + side * capacity).astype(jnp.bfloat16)
    ids = lax.dot_general(named, into, contract_last, preferred_element_type=jnp.float32)
    return placed, ids, within


def place_kernel(groups, spot_ref, *refs):
    sources, (half_ref, ids_ref, plan_ref), held, done = refs[:3], refs[3:6], refs[6:9], refs[9]
    copies = [
        pltpu.make_async_copy(source, kept, done.at[i])
        for i, (source, kept) in enumerate(zip(sources, held))
    ]
    for copy in copies[::-1]:
        copy.start()
    for copy in copies[::-1]:
        copy.wait()
    placed, ids, within = put_rows(groups, 0, spot_ref, *held)
    teams, count, _ = half_ref.shape
    for start in range(0, count // capacity * lanes, 4 * wide):
        values = placed(start, 4 * wide)
        for shift in range(0, 4 * wide, lanes):
            at = (start + shift) // lanes * capacity
            half_ref[:, at : at + capacity, :] = values[:, shift : shift + lanes].reshape(
                teams, capacity, lanes
            )
    ids_ref[...] = ids
    owner = held[1][...]
    plan_ref[0:1, :] = owner >> core_bits
    plan_ref[1:2, :] = within + (owner & (cores - 1)) * capacity


def pair_kernel(
    groups, spot_ref, emb_ref, owner_ref, cluster_ref, half_ref, ids_ref, main_ref, last_ref
):
    placed, ids, _ = put_rows(groups, 1, spot_ref, emb_ref, owner_ref, cluster_ref)
    teams, count, _ = half_ref.shape
    border = main_ref.shape[1] - note

    def store(at, values):
        if at < border:
            main_ref[:, at : at + capacity, :] = values
        else:
            last_ref[:, at - border : at - border + capacity, :] = values

    for start in range(0, count // capacity * lanes, 4 * wide):
        values = placed(start, 4 * wide)
        for shift in range(0, 4 * wide, lanes):
            block = (start + shift) // lanes
            store(block * field, half_ref[:, block * capacity : (block + 1) * capacity, :])
            store(
                block * field + capacity,
                values[:, shift : shift + lanes].reshape(teams, capacity, lanes),
            )
    ids = (ids + ids_ref[...] - 1.0).astype(jnp.bfloat16)
    main_ref[:, border:, :] = jnp.broadcast_to(
        ids[:, None, :], (teams, note, lanes)
    )


def read_ids(ref, hold):
    count = lanes // field
    blocks = ref.shape[0] // count
    hold[...] = jnp.max(ref[:, ref.shape[1] - note :, :].astype(jnp.float32), axis=1)
    lane = lax.broadcasted_iota(jnp.int32, (blocks, lanes), 1)
    total = hold[pl.ds(0, blocks, stride=count), :]
    for q in range(1, count):
        piece = pltpu.roll(hold[pl.ds(q, blocks, stride=count), :], field * q, 1)
        total = jnp.where(lane >> field_bits == q, piece, total)
    return total


def features(refs, blocks, start, count):
    teams = slice(start // field, (start + count) // field)
    found = []
    for block in blocks:
        low, high = block * field, (block + 1) * field
        parts = []
        if low < first_rows:
            parts.append(refs[0][teams, low : min(high, first_rows), :])
        if high > first_rows:
            parts.append(refs[1][teams, max(low, first_rows) - first_rows : high - first_rows, :])
        piece = parts[0] if len(parts) == 1 else jnp.concatenate(parts, axis=1)
        found.append(piece.reshape(count, lanes))
    return jnp.concatenate(found, axis=1)


def to_column(row):
    return jnp.transpose(jnp.broadcast_to(row, (lanes, lanes)))


def columns_of(ids):
    return jnp.concatenate([to_column(ids[b : b + 1, :]) for b in range(ids.shape[0])], axis=0)


def to_rows(tile):
    return jnp.concatenate(
        [
            jnp.max(jnp.transpose(tile[b * lanes : (b + 1) * lanes, :]), axis=0, keepdims=True)
            for b in range(tile.shape[0] // lanes)
        ],
        axis=0,
    )


def product(left, right):
    return lax.dot_general(left, right, contract_last, preferred_element_type=jnp.float32)


def own_kernel(main, last, plan_ref, out_ref, onehot_ref, pick_ref, hold):
    team = lax.broadcasted_iota(jnp.int32, pick_ref.shape, 0)
    onehot = (team == plan_ref[0:1, :]).astype(jnp.bfloat16)
    onehot_ref[...] = jnp.concatenate([onehot] * 3, axis=0)
    pick_ref[...] = jnp.where(team == plan_ref[1:2, :], 1.0, 0.0)
    ids = read_ids(main, hold)
    rows = ids.shape[0] * lanes
    blocks = range((first_rows + last.shape[1]) // field)
    columns = columns_of(ids)
    left = features((main, last), blocks, 0, rows)
    steps, per = rows // wide, wide // lanes
    best, tops = [None] * steps, []
    for at in range(steps):
        begin = at * wide
        masked = []
        total = product(left[begin:, :], left[begin : begin + wide, :])
        for h in range(per):
            scores = total[:, h * lanes : (h + 1) * lanes]
            row_ids = ids[at * per + h : at * per + h + 1, :]
            row = lax.broadcasted_iota(jnp.int32, scores.shape, 0)
            column = lax.broadcasted_iota(jnp.int32, scores.shape, 1)
            same = columns[begin:, :] == jnp.where(row_ids < 0, -2.0, row_ids)
            masked.append(jnp.where(same & (row - column != h * lanes), scores, -1.0))
            tops.append(jnp.max(masked[-1], axis=0, keepdims=True))
        both = jnp.maximum(masked[0], masked[1])
        for i in range(at, steps):
            part = both[i * wide - begin : (i + 1) * wide - begin, :]
            best[i] = part if best[i] is None else jnp.maximum(best[i], part)
    out_ref[...] = jnp.maximum(
        to_rows(jnp.concatenate(best, axis=0)), jnp.concatenate(tops, axis=0)
    )


def masked_sums(sums, left_ids, right_ids):
    return jnp.concatenate(
        [
            jnp.where(
                left_ids == jnp.where(right_ids[h : h + 1, :] < 0, -2.0, right_ids[h : h + 1, :]),
                sums[:, h * lanes : (h + 1) * lanes],
                nowhere,
            )
            for h in range(wide // lanes)
        ],
        axis=1,
    )


def start_kernel(spot_ref, main, after, before, near_ref, side_ref, hold):
    low = spot_ref[1] == 1
    ids, after_ids, before_ids = [
        read_ids(ref, hold.at[i]) for i, ref in enumerate((main, after, before))
    ]
    count = ids.shape[0]
    rows = count * lanes
    half = rows // 2
    columns = columns_of(ids)
    right_ids = jnp.where(low, after_ids, before_ids)
    left_ids = jnp.where(low, before_ids[: count // 2, :], after_ids[count // 2 :, :])
    left_columns = columns_of(left_ids)
    blocks = range(early)
    left = features((main,), blocks, 0, rows)
    side_left = jnp.where(
        low, features((before,), blocks, 0, half), features((after,), blocks, half, half)
    )
    per = wide // lanes
    for at in range(rows // wide):
        span, cut = slice(at * wide, (at + 1) * wide), slice(at * per, (at + 1) * per)
        near = features((after,), blocks, at * wide, wide)
        near_ref[:, span] = masked_sums(product(left, near), columns, after_ids[cut, :])
        right = jnp.where(low, near, features((before,), blocks, at * wide, wide))
        side_ref[:, span] = masked_sums(
            product(side_left, right), left_columns, right_ids[cut, :]
        )


def add_block(total, best):
    halves = [total[:, h * lanes : (h + 1) * lanes] for h in range(wide // lanes)]
    for part in halves:
        best = part if best is None else jnp.maximum(best, part)
    return best, [jnp.max(part, axis=0, keepdims=True) for part in halves]


def cross_kernel(
    spot_ref,
    main,
    last,
    after_main,
    after_last,
    before_main,
    before_last,
    near_ref,
    side_ref,
    inside_ref,
    out_ref,
    table,
):
    low = spot_ref[1] == 1
    blocks = inside_ref.shape[0]
    rows = blocks * lanes
    half = rows // 2
    late = range(early, (first_rows + last.shape[1]) // field)
    left, after, before = [
        features(refs, late, 0, rows)
        for refs in ((main, last), (after_main, after_last), (before_main, before_last))
    ]
    side_left = jnp.where(low, before[:half, :], after[half:, :])
    best, far, up, side = None, None, [], []
    for at in range(rows // wide):
        span = slice(at * wide, (at + 1) * wide)
        near = after[span, :]
        right = jnp.where(low, near, before[span, :])
        best, tops = add_block(near_ref[:, span] + product(left, near), best)
        up += tops
        far, tops = add_block(side_ref[:, span] + product(side_left, right), far)
        side += tops
    up, side = jnp.concatenate(up, axis=0), jnp.concatenate(side, axis=0)
    mine = jnp.maximum(to_rows(best), inside_ref[...])
    found = to_rows(far)
    blank = jnp.full(found.shape, -1.0, jnp.float32)
    placed = jnp.where(
        low, jnp.concatenate([found, blank], axis=0), jnp.concatenate([blank, found], axis=0)
    )
    up = jnp.maximum(up, jnp.where(low, side, placed))
    down = jnp.where(low, placed, side)
    count = lanes // field
    steps = (0, 1, places - 1)
    for step, values in enumerate((mine, up, down)):
        for q in range(count):
            turned = values if q == 0 else pltpu.roll(values, lanes - field * q, 1)
            table[step, pl.ds(q, blocks, stride=count), :] = turned
    core, x, y = spot_ref[0], spot_ref[2], spot_ref[3]
    each = places * depth
    across = cores * places

    def found(step, other):
        values = table[step]
        return jnp.where(other == core, values, pltpu.roll(values, lanes - capacity, 1))

    @pl.when(core == 0)
    def _():
        for step, move in enumerate(steps):
            for other in range(cores):
                start = other * places + lax.rem(x + move, places)
                out_ref[pl.ds(start, each, stride=across), :] = found(step, other)

    @pl.when(core == 1)
    def _():
        for step, move in enumerate(steps):
            row = lax.rem(y + move, places) * (depth * across)
            for other in range(cores):
                values = found(step, other)
                for place in range(places):
                    start = row + other * places + place
                    out_ref[pl.ds(start, depth, stride=across), :] = values[
                        place * depth : (place + 1) * depth, :
                    ]


def fetch_kernel(spot_ref, back_ref, onehot_ref, pick_ref, out_ref):
    x, y = spot_ref[2], spot_ref[3]
    each = places * depth
    across = cores * places
    even, odd = None, []
    for move in (0, 1, places - 1):
        rows = back_ref[pl.ds(lax.rem(x + move, places), each, stride=across), :]
        even = rows if even is None else jnp.maximum(even, rows)
    for place in range(places):
        total = None
        for move in (0, 1, places - 1):
            start = lax.rem(y + move, places) * (depth * across) + places + place
            rows = back_ref[pl.ds(start, depth, stride=across), :]
            total = rows if total is None else jnp.maximum(total, rows)
        odd.append(total)
    odd = pltpu.roll(jnp.concatenate(odd, axis=0), capacity, 1)
    rest = jnp.where(lax.broadcasted_iota(jnp.int32, even.shape, 1) < capacity, even, odd)
    rest = jnp.where(lax.broadcasted_iota(jnp.int32, even.shape, 1) < field, rest, 0.0)
    pieces = []
    for _ in range(3):
        pieces.append(rest.astype(jnp.bfloat16))
        rest = rest - pieces[-1].astype(jnp.float32)
    found = lax.dot_general(
        jnp.concatenate(pieces, axis=0),
        onehot_ref[...],
        (((0,), (0,)), ((), ())),
        preferred_element_type=jnp.float32,
    )[:field, :]
    out_ref[...] = jnp.sum(jnp.where(pick_ref[...] > 0, found, 0.0), axis=0, keepdims=True)


def send(values, route):
    return lax.ppermute(values, everyone, route)


def trade(values, teams):
    return lax.all_to_all(
        values, everyone, split_axis=0, concat_axis=0, axis_index_groups=teams, tiled=True
    )


def shards(embeddings, owner, cluster):
    rows, width = embeddings.shape
    groups = lax.axis_size("ingest")
    spots = groups * capacity
    blocks = spots // lanes
    each = places * depth
    f32 = jnp.float32
    at, x = lax.axis_index("ingest"), lax.axis_index("span")
    core, y = at % cores, at // (cores * depth)
    low = jnp.where(core == 0, x, y) < places // 2
    spot = jnp.stack([core, low.astype(jnp.int32), x, y]).astype(jnp.int32)
    smem, vmem = pl.BlockSpec(memory_space=pltpu.SMEM), pl.BlockSpec(memory_space=pltpu.VMEM)

    def call(kernel, out_shape, name, *args, scratch=()):
        return pl.pallas_call(
            kernel,
            out_shape=out_shape,
            in_specs=[smem if a is spot else vmem for a in args],
            scratch_shapes=scratch,
            compiler_params=params(),
            name=name,
        )(*args)

    def array(*shape, dtype=jnp.bfloat16):
        return jax.ShapeDtypeStruct(shape, dtype)

    swap = other_core()
    sources = embeddings, owner.reshape(1, rows), cluster.reshape(1, rows)
    others = [send(values, swap) for values in sources]
    total = width // lanes * field
    half, ids, plan = pl.pallas_call(
        functools.partial(place_kernel, groups),
        out_shape=[
            array(each, total // cores, lanes),
            array(each, lanes, dtype=f32),
            array(2, rows, dtype=jnp.int32),
        ],
        in_specs=[smem] + [pl.BlockSpec(memory_space=pltpu.HBM)] * 3,
        scratch_shapes=[pltpu.VMEM(values.shape, values.dtype) for values in sources]
        + [pltpu.SemaphoreType.DMA((3,))],
        compiler_params=params(),
        name="place",
    )(spot, *[pltpu.with_memory_space_constraint(values, pltpu.HBM) for values in sources])
    parts = call(
        functools.partial(pair_kernel, groups),
        [array(each, first_rows + note, lanes), array(each, total - first_rows, lanes)],
        "pair",
        spot,
        *others,
        half,
        ids,
    )
    teams = plane_teams()
    own, after, before = [], [], []
    for part in parts:
        got = trade(part, teams)
        own.append(got)
        after.append(send(got, beside(-1)))
        before.append(send(got, beside(1)))
    held = pltpu.VMEM((each, lanes), f32)
    inside, onehot, pick = call(
        own_kernel,
        [array(blocks, lanes, dtype=f32), array(3 * each, rows), array(each, rows, dtype=f32)],
        "own",
        *own,
        plan,
        scratch=[held],
    )
    near, side = call(
        start_kernel,
        [array(spots, spots, dtype=f32), array(spots // 2, spots, dtype=f32)],
        "start",
        spot,
        own[0],
        after[0],
        before[0],
        scratch=[pltpu.VMEM((3, each, lanes), f32)],
    )
    count = groups * places
    best = call(
        cross_kernel,
        array(count, lanes, dtype=f32),
        "cross",
        spot,
        *own,
        *after,
        *before,
        near,
        side,
        inside,
        scratch=[pltpu.VMEM((3, each, lanes), f32)],
    )
    back = lax.all_to_all(
        best.reshape(count, 1, 1, lanes), everyone, split_axis=0, concat_axis=0, tiled=True
    ).reshape(count, lanes)
    result = call(fetch_kernel, array(1, rows, dtype=f32), "fetch", spot, back, onehot, pick)
    return result.reshape(rows)


def solution(mesh):
    placed = (P(("ingest", "span"), None), P(("ingest", "span"), None), P(("ingest", "span")))
    return jax.shard_map(
        shards, mesh=mesh, in_specs=placed, out_specs=P(("ingest", "span")), check_vma=False
    )
```
